512 devices in a mesh: region: 128 (over x, z, core), chan: 4 (over y).
Axes of the slice: x: 4, y: 4, z: 16, core: 2. Of those that a mesh axis runs over, the one named last changes fastest.
Arguments:
- sky_maps: bfloat16 [128, 65536], P('chan', 'region'), may hold values from -6 to 6
- neighbours: int32 [8, 65536], P(None, 'region'), may hold values from 0 to 768, as said below
- send_lists: int32 [2, 16384], P(None, 'region'), may hold values from 0 to 511, as said below
- counts: int32 [128], replicated, may hold values from 171 to 511, as said below
- cheb_weight: bfloat16 [4, 128, 128], P(None, 'chan'), may hold values from -0.25 to 0.25
- first_weight: bfloat16 [128, 512], P(None, 'chan'), may hold values from -0.5 to 0.5
- second_weight: bfloat16 [512, 64], P('chan'), may hold values from -0.25 to 0.25
- cotangent: bfloat16 [64, 32768], P('chan', 'region'), may hold values from -6 to 6
Outputs:
- mlp_out: bfloat16 [64, 32768], P('chan', 'region')
- input_grad: float32 [128, 65536], P('chan', 'region')
- cheb_grad: float32 [4, 128, 128], P(None, 'chan')
- first_grad: float32 [128, 512], P(None, 'chan')
- second_grad: float32 [512, 64], P('chan')
The draws below stay inside these ranges and needn't reach their ends.
Inputs may be any that keep to these rules, and one draw needn't show every extreme that they name: Patch i observes its pixel slots 0 to counts[i] - 1 and no others; the counts sum to 32768. Column p of patch i lists up to eight neighbours of slot p in the encoding of the operator P; links join observed slots only and are symmetric, across patches too. `send_lists`: each row of a patch's send lists holds 128 distinct slots of that patch.
All inputs are finite; a program needn't handle non-finite values.
Results may differ from the reference program's by a relative error of at most 0.025.
Values may be sent and summed in bfloat16 or wider, within the bound.
A program may use at most 64 MiB of HBM per device.

```python
import math
import jax
import jax.numpy as jnp
from jax import lax

CIN = 128
COUT = 128
HID = 512
OUT = 64
K = 4
WW = 128
OBS_DEV = 256
PIX = 512
NPIXT = 65536
ROWS = 32768
N_REGION = 128
N_CHAN = 4


def footprint(key):
    base = jax.random.fold_in(key, 17)
    key_lift, key_forced, key_heavy, key_order = jax.random.split(base, 4)
    groups = N_REGION // 4
    lift_max = OBS_DEV // 3
    lift = jax.random.randint(key_lift, (groups,), 0, lift_max + 1)
    forced = jax.random.randint(key_forced, (), 0, groups)
    lift = jnp.where(jnp.arange(groups) == forced, lift_max, lift)
    heavy = jax.random.randint(key_heavy, (groups,), 0, 4)
    is_heavy = jnp.arange(4)[None, :] == heavy[:, None]
    counts = (OBS_DEV + jnp.where(is_heavy, 3 * lift[:, None], -lift[:, None])).reshape(-1).astype(jnp.int32)
    order_keys = jax.random.split(key_order, N_REGION + 1)
    orders = jax.vmap(lambda sub_key: jax.random.permutation(sub_key, PIX))(order_keys[:N_REGION]).astype(jnp.int32)
    middle = (2 + jax.random.permutation(order_keys[N_REGION], PIX - 3)).astype(jnp.int32)
    first_order = jnp.concatenate([jnp.array([0, 1], jnp.int32), middle, jnp.array([PIX - 1], jnp.int32)])
    orders = jnp.where(jnp.arange(N_REGION)[:, None] == 0, first_order[None, :], orders)
    device_rows = jnp.broadcast_to(jnp.arange(N_REGION, dtype=jnp.int32)[:, None], (N_REGION, PIX))
    slot_ids = jnp.broadcast_to(jnp.arange(PIX, dtype=jnp.int32)[None, :], (N_REGION, PIX))
    slots = jnp.zeros((N_REGION, PIX), jnp.int32).at[device_rows, orders].set(slot_ids)
    seen = slots < counts[:, None]
    return (counts, orders, slots, seen)


def draw_counts(key, part):
    return footprint(key)[0]


def draw_send_lists(key, part):
    counts, orders, slots, seen = footprint(key)
    lower_list = slots[:, :WW]
    upper_list = slots[:, PIX - WW:]
    return jnp.stack([lower_list, upper_list]).reshape(2, N_REGION * WW).astype(jnp.int32)


def draw_neighbours(key, part):
    counts, orders, slots, seen = footprint(key)
    grid_rows = PIX // WW
    row_of = orders // WW
    col_of = orders % WW
    self_seen = jnp.arange(PIX, dtype=jnp.int32)[None, :] < counts[:, None]
    no_link = PIX + 2 * WW
    blank = jnp.zeros((1, PIX), bool)
    seen_below = jnp.concatenate([blank, seen[:-1]], axis=0)
    seen_above = jnp.concatenate([seen[1:], blank], axis=0)
    entries = []
    for step_row in (-1, 0, 1):
        for step_col in (-1, 0, 1):
            if step_row == 0 and step_col == 0:
                continue
            near_row = row_of + step_row
            near_col = col_of + step_col
            col_fine = (near_col >= 0) & (near_col < WW)
            safe_col = jnp.clip(near_col, 0, WW - 1)
            inner_cell = jnp.clip(near_row, 0, grid_rows - 1) * WW + safe_col
            inner_slot = jnp.take_along_axis(slots, inner_cell, axis=1)
            inner_seen = jnp.take_along_axis(seen, inner_cell, axis=1)
            lower_seen = jnp.take_along_axis(seen_below, (grid_rows - 1) * WW + safe_col, axis=1)
            upper_seen = jnp.take_along_axis(seen_above, safe_col, axis=1)
            is_lower = near_row < 0
            is_upper = near_row >= grid_rows
            target = jnp.where(is_lower, PIX + safe_col, jnp.where(is_upper, PIX + WW + safe_col, inner_slot))
            linked = col_fine & self_seen & jnp.where(is_lower, lower_seen, jnp.where(is_upper, upper_seen, inner_seen))
            entries.append(jnp.where(linked, target, no_link))
    return jnp.stack(entries).reshape(8, N_REGION * PIX).astype(jnp.int32)


def steps_of(rng, dims, cuts, low, top_value):
    gain, own = 1.0, jax.random.fold_in(rng, 6)
    for dim, shards_of in cuts:
        draws = jnp.exp(jax.random.uniform(jax.random.fold_in(own, dim), (shards_of,), jnp.float32, low / len(cuts), top_value / len(cuts)))
        gain = gain * jnp.repeat(draws, dims[dim] // shards_of).reshape([-1 if axis == dim else 1 for axis in range(len(dims))])
    return gain


def scatter_about(stream_key, shape, deviation, limit, shards=(), kind=jnp.bfloat16):
    values = deviation * jax.random.normal(stream_key, shape, jnp.float32)
    if shards:
        values = values * steps_of(stream_key, shape, shards, -0.22, 0.18)
    return jnp.clip(values, -limit, limit).astype(kind)


def setup_inputs(seed: int = 0) -> dict:
    streams_of = jax.random.split(jax.random.key(seed), 9)
    return {
        "sky_maps": scatter_about(streams_of[0], (CIN, NPIXT), 1.0, 6.0, ((0, 4), (1, 128))),
        "neighbours": draw_neighbours(jax.random.fold_in(streams_of[8], 71), 0),
        "send_lists": draw_send_lists(jax.random.fold_in(streams_of[8], 71), 0),
        "counts": draw_counts(jax.random.fold_in(streams_of[8], 71), 0),
        "cheb_weight": scatter_about(streams_of[4], (K, CIN, COUT), (K * CIN) ** -0.5, 0.25, ((1, 4),)),
        "first_weight": scatter_about(streams_of[5], (COUT, HID), COUT ** -0.5, 0.5, ((1, 4),)),
        "second_weight": scatter_about(streams_of[6], (HID, OUT), HID ** -0.5, 0.25, ((0, 4),)),
        "cotangent": scatter_about(streams_of[7], (OUT, ROWS), 1.0, 6.0, ((0, 4), (1, 128))),
    }


def neighbour_sum(values, inv_root, neighbours3, send3):
    channels = values.shape[0]
    scaled = values * inv_root[None]
    flat_scaled = scaled.reshape(channels, N_REGION * PIX)
    device_base = (jnp.arange(N_REGION, dtype=jnp.int32) * PIX)[:, None]
    to_lower = jnp.take(flat_scaled, (send3[0] + device_base).reshape(-1), axis=1).reshape(channels, N_REGION, WW)
    to_upper = jnp.take(flat_scaled, (send3[1] + device_base).reshape(-1), axis=1).reshape(channels, N_REGION, WW)
    empty_rim = jnp.zeros((channels, 1, WW), values.dtype)
    from_lower = jnp.concatenate([empty_rim, to_upper[:, :-1]], axis=1)
    from_upper = jnp.concatenate([to_lower[:, 1:], empty_rim], axis=1)
    ext_len = PIX + 2 * WW + 1
    extended = jnp.concatenate([scaled, from_lower, from_upper, jnp.zeros((channels, N_REGION, 1), values.dtype)], axis=2)
    extended = extended.reshape(channels, N_REGION * ext_len)
    ext_base = (jnp.arange(N_REGION, dtype=jnp.int32) * ext_len)[None, :, None]
    positions = (neighbours3 + ext_base).reshape(neighbours3.shape[0], N_REGION * PIX)
    summed = jnp.take(extended, positions[0], axis=1)
    for position in range(1, neighbours3.shape[0]):
        summed = summed + jnp.take(extended, positions[position], axis=1)
    return -inv_root[None] * summed.reshape(channels, N_REGION, PIX)

def chebyshev_basis(start_maps, inv_root, neighbours3, send3):
    terms = [start_maps, neighbour_sum(start_maps, inv_root, neighbours3, send3)]
    for level in range(2, K):
        terms.append(2.0 * neighbour_sum(terms[-1], inv_root, neighbours3, send3) - terms[-2])
    return jnp.stack(terms)

def reference(sky_maps, neighbours, send_lists, counts, cheb_weight, first_weight, second_weight, cotangent):
    neighbours3 = neighbours.reshape(neighbours.shape[0], N_REGION, PIX)
    send3 = send_lists.reshape(2, N_REGION, WW)
    degree = lax.optimization_barrier(jnp.sum((neighbours3 != PIX + 2 * WW).astype(jnp.float32), axis=0))
    inv_root = 1.0 / jnp.sqrt(jnp.maximum(degree, 1.0))
    per_group = CIN // N_CHAN
    sub_width = math.gcd(per_group, 8)
    sub_count = per_group // sub_width
    maps3 = sky_maps.reshape(CIN, N_REGION, PIX)

    def basis_of(block_id):
        start_maps = lax.dynamic_slice_in_dim(maps3, block_id * sub_width, sub_width, 0).astype(jnp.float32)
        return chebyshev_basis(start_maps, inv_root, neighbours3, send3)

    def rounded_of(basis):
        return lax.optimization_barrier(basis.astype(jnp.bfloat16)).astype(jnp.float32)

    def weight_of(block_id):
        return lax.dynamic_slice_in_dim(cheb_weight, block_id * sub_width, sub_width, 1).astype(jnp.float32)

    def group_step(accum, group_id):

        def block_step(partial_value, inner):
            block_id = group_id * sub_count + inner
            basis = rounded_of(basis_of(block_id))
            return (partial_value + jnp.einsum('kcnp,kco->onp', basis, weight_of(block_id)), None)
        partial_value, unused = lax.scan(block_step, jnp.zeros((COUT, N_REGION, PIX), jnp.float32), jnp.arange(sub_count, dtype=jnp.int32))
        return (accum + lax.optimization_barrier(partial_value.astype(jnp.bfloat16)).astype(jnp.float32), None)
    accum, unused = lax.scan(group_step, jnp.zeros((COUT, N_REGION, PIX), jnp.float32), jnp.arange(N_CHAN, dtype=jnp.int32))
    conv = accum.astype(jnp.bfloat16).reshape(COUT, N_REGION * PIX)
    out_col = jnp.arange(N_REGION * OBS_DEV, dtype=jnp.int32)
    global_row = out_col % OBS_DEV * N_REGION + out_col // OBS_DEV
    ends = jnp.cumsum(counts).astype(jnp.int32)
    starts = ends - counts
    source = jnp.searchsorted(ends, global_row, side='right').astype(jnp.int32)
    columns = source * PIX + global_row - jnp.take(starts, source)
    features = jnp.take(conv, columns, axis=1)
    hid_share = HID // N_CHAN
    grad_scale = 1.0 / math.sqrt(N_REGION * OBS_DEV)

    def head_step(state_pair, group_id):
        out_sum, feat_sum = state_pair
        first_part = lax.dynamic_slice_in_dim(first_weight, group_id * hid_share, hid_share, 1)
        second_part = lax.dynamic_slice_in_dim(second_weight, group_id * hid_share, hid_share, 0)
        pre_act = jnp.dot(first_part.T, features, preferred_element_type=jnp.float32)
        gate_val = jax.nn.sigmoid(pre_act)
        hidden = (pre_act * gate_val).astype(jnp.bfloat16)
        out_part = jnp.dot(second_part.T, hidden, preferred_element_type=jnp.float32)
        out_sum = out_sum + lax.optimization_barrier(out_part.astype(jnp.bfloat16)).astype(jnp.float32)
        d_hidden = jnp.dot(second_part, cotangent, preferred_element_type=jnp.float32)
        d_pre = (d_hidden * gate_val * (1.0 + pre_act * (1.0 - gate_val))).astype(jnp.bfloat16)
        second_piece = jnp.dot(hidden, cotangent.T, preferred_element_type=jnp.float32)
        first_piece = jnp.dot(features, d_pre.T, preferred_element_type=jnp.float32)
        feat_part = jnp.dot(first_part, d_pre, preferred_element_type=jnp.float32)
        feat_sum = feat_sum + lax.optimization_barrier(feat_part.astype(jnp.bfloat16)).astype(jnp.float32)
        return ((out_sum, feat_sum), (first_piece, second_piece))
    start_pair = (jnp.zeros((OUT, N_REGION * OBS_DEV), jnp.float32), jnp.zeros((COUT, N_REGION * OBS_DEV), jnp.float32))
    (out_sum, feat_sum), (first_parts, second_parts) = lax.scan(head_step, start_pair, jnp.arange(N_CHAN, dtype=jnp.int32))
    mlp_out = out_sum.astype(jnp.bfloat16)
    first_grad = jnp.transpose(first_parts, (1, 0, 2)).reshape(COUT, HID) * grad_scale
    second_grad = second_parts.reshape(HID, OUT) * grad_scale
    d_features = feat_sum.astype(jnp.bfloat16)
    d_conv = jnp.zeros((COUT, N_REGION * PIX), jnp.float32).at[:, columns].set(d_features.astype(jnp.float32))
    d_conv = d_conv.reshape(COUT, N_REGION, PIX)

    def back_block(block_id):
        rounded = rounded_of(basis_of(block_id))
        weight_part = weight_of(block_id)
        d_basis = jnp.einsum('kco,onp->kcnp', weight_part, d_conv)
        cheb_part = jnp.einsum('kcnp,onp->kco', rounded, d_conv)
        adjoint = [d_basis[level] for level in range(K)]
        for level in range(K - 1, 1, -1):
            adjoint[level - 1] = adjoint[level - 1] + 2.0 * neighbour_sum(adjoint[level], inv_root, neighbours3, send3)
            adjoint[level - 2] = adjoint[level - 2] - adjoint[level]
        grad_block = adjoint[0] + neighbour_sum(adjoint[1], inv_root, neighbours3, send3)
        return (grad_block, cheb_part)
    grads_in, cheb_parts = lax.map(back_block, jnp.arange(CIN // sub_width, dtype=jnp.int32))
    input_grad = grads_in.reshape(CIN, N_REGION * PIX)
    cheb_grad = jnp.transpose(cheb_parts, (1, 0, 2, 3)).reshape(K, CIN, COUT) * grad_scale
    return (mlp_out, input_grad, cheb_grad, first_grad, second_grad)
```

```python
import math

import jax
import jax.numpy as jnp
from jax import lax
from jax.experimental import pallas as pl
from jax.experimental.pallas import tpu as pltpu
from jax.sharding import PartitionSpec as P

F32, BF16, I32 = jnp.float32, jnp.bfloat16, jnp.int32
MESH = pl.DeviceIdType.MESH
PIX, WW, ORDER, GROUP = 512, 128, 4, 32
NZ, NXC, NCHAN, NREGION = 16, 8, 4, 128
TILES = 5
STRIDE = 3
OUT_PART, ROWS_DEV, OUTF = 16, 256, 64

W1, W2, A1, A2, CT, CP, DG, GS, MO, B1, B2, G1, F2, EXCHANGES = range(14)


def dot(left, right, left_dim=1, right_dim=0):
    return lax.dot_general(
        left, right, (((left_dim,), (right_dim,)), ((), ())), preferred_element_type=F32
    )


def iota(shape, dim):
    return lax.broadcasted_iota(I32, shape, dim)


def kernel(
    sky, nb, sl, cnt, cheb, w1, w2, cot,
    mo_out, ig_out, cg_out, fg_out, sg_out,
    amat, smat, mmat, basis, hs, hr, wg1, wg2, s1, r1, s2, r2, cs, ct, cp, cr, dhid,
    dg_s, dg, gs, gr, ms, mr, g1, rg1, hbuf, rg2, ft, rf, fin,
    hsend, hrecv, send, recv, g2send, g2recv, f1send, f1recv,
):
    region, chan = lax.axis_index("region"), lax.axis_index("chan")
    core, z, x = lax.rem(region, 2), lax.rem(lax.div(region, 2), NZ), lax.div(region, 2 * NZ)
    xc = x * 2 + core

    def z_device(zz):
        return ((x * NZ + zz) * 2 + core, chan)

    def z_peer(step):
        other = lax.rem(z + step, NZ)
        return other, z_device(other)

    def xc_peer(step):
        other = lax.rem(xc + step, NXC)
        return other, ((lax.div(other, 2) * NZ + z) * 2 + lax.rem(other, 2), chan)

    def chan_peer(step):
        other = lax.rem(chan + step, NCHAN)
        return other, (region, other)

    lower = (lax.rem(region + NREGION - 1, NREGION), chan)
    upper = (lax.rem(region + 1, NREGION), chan)

    barrier = pltpu.get_barrier_semaphore()

    def greet(peer, count):
        def step(d, carry):
            pl.semaphore_signal(barrier, inc=1, device_id=peer(d)[1], device_id_type=MESH)
            return carry

        lax.fori_loop(1, count, step, 0)

    for device in (lower, upper):
        pl.semaphore_signal(barrier, inc=1, device_id=device, device_id_type=MESH)
    greet(chan_peer, NCHAN)
    greet(xc_peer, NXC)
    greet(z_peer, NZ)

    def spread(key, peer, count, src_at, dst):
        def step(d, carry):
            slot, device = peer(d)
            pltpu.make_async_remote_copy(
                src_ref=src_at(slot), dst_ref=dst, send_sem=send.at[key],
                recv_sem=recv.at[key], device_id=device, device_id_type=MESH,
            ).start()
            return carry

        lax.fori_loop(1, count, step, 0)

    def await_bytes(ref, sem):
        pltpu.make_async_copy(ref, ref, sem).wait()

    links = nb[...]
    inv = 1.0 / jnp.sqrt(
        jnp.maximum(jnp.sum((links != PIX + 2 * WW).astype(F32), axis=0, keepdims=True), 1.0)
    )
    slot_row = iota((PIX, WW), 0)
    for side in range(2):
        smat[:, side * WW : (side + 1) * WW] = (
            jnp.where(slot_row == sl[side : side + 1, :], 1.0, 0.0).astype(BF16)
        )

    def halo_copy(step, side):
        return pltpu.make_async_remote_copy(
            src_ref=hs.at[step, side], dst_ref=hr.at[step, 1 - side],
            send_sem=hsend.at[step, side], recv_sem=hrecv.at[step, 1 - side],
            device_id=(lower, upper)[side], device_id_type=MESH,
        )

    def rim(step, values):
        scaled = values * inv
        high = scaled.astype(BF16)
        edge = dot(high, smat[...]).astype(BF16)
        hs[step, 0] = edge[:, :WW]
        hs[step, 1] = edge[:, WW:]
        return scaled, high

    def halo_start(step):
        for side in range(2):
            halo_copy(step, side).start()

    def inner(pair):
        scaled, high = pair
        low = (scaled - high.astype(F32)).astype(BF16)
        both = dot(jnp.concatenate([high, low], axis=0), amat[:PIX])
        return both[:GROUP] + both[GROUP:]

    def finish(step, local):
        for side in range(2):
            halo_copy(step, 1 - side).wait_recv()
        local = local + dot(hr[step, 0], amat[PIX : PIX + WW])
        local = local + dot(hr[step, 1], amat[PIX + WW :])
        return -inv * local

    v0 = sky[...].astype(F32)
    basis[0:GROUP] = sky[...]
    pair = rim(0, v0)

    pl.semaphore_wait(barrier, 2 + (NCHAN - 1) + (NXC - 1) + (NZ - 1))
    halo_start(0)

    lane, row = iota((NREGION, NREGION), 1), iota((NREGION, NREGION), 0)
    counts = cnt[...].astype(F32)
    zmajor = ((((row & 7) >> 1) * NZ + (row >> 3)) * 2) + (row & 1)
    xcmajor = (((row >> 5) * NZ + (row & 15)) * 2) + ((row >> 4) & 1)
    own_start = jnp.sum(
        jnp.where(lane < region, counts, 0.0), axis=1, keepdims=True
    ).astype(I32)

    def places(order):
        count = jnp.sum(jnp.where(lane == order, counts, 0.0), axis=1, keepdims=True).astype(I32)
        start = jnp.sum(jnp.where(lane < order, counts, 0.0), axis=1, keepdims=True).astype(I32)
        off = (region - start) & (NREGION - 1)
        first = (start + off - region) >> 7
        return count, off, first

    def exchange1(k, key, message):
        s1[k] = message.reshape(NZ, NXC, 128)
        spread(key, z_peer, NZ, lambda slot: s1.at[k, slot], r1.at[k, z])
        r1[k, z] = s1[k, z]

    def exchange2(k, key1, key2):
        await_bytes(r1.at[k, pl.ds(0, NZ - 1)], recv.at[key1])
        for d in range(NXC):
            s2[k, d] = r1[k, :, d, :].astype(BF16)
        spread(key2, xc_peer, NXC, lambda slot: s2.at[k, slot], r2.at[k, xc])
        r2[k, xc] = s2[k, xc]

    def arrived2(k, key2):
        await_bytes(r2.at[k, pl.ds(0, NXC - 1)], recv.at[key2])
        return r2[k].reshape(NREGION, 128).astype(F32).T

    count1, off1, first1 = places(zmajor)
    own_cot = cot[...].astype(F32)
    shifted = [own_cot] + [pltpu.roll(own_cot, ROWS_DEV - s, 1) for s in range(1, 4)]
    shifted = jnp.concatenate(shifted + [jnp.zeros((64, ROWS_DEV), F32)], axis=0).astype(BF16)
    choice = jnp.where(iota((NREGION, ROWS_DEV), 1) == first1, 1.0, 0.0).astype(BF16)
    message = dot(choice, shifted, 1, 1)
    message = jnp.where((lane >> 4) * NREGION + off1 < count1, message, 0.0)
    exchange1(0, A1, message)
    spread(W1, chan_peer, NCHAN, lambda slot: w1, wg1.at[chan])
    spread(W2, chan_peer, NCHAN, lambda slot: w2, wg2.at[chan])

    gone = jnp.where(region == 0, 0, -1)
    gone_up = jnp.where(region == NREGION - 1, 0, -1)
    links = jnp.where((links >= PIX) & (links < PIX + WW) & (gone == 0), PIX + 2 * WW, links)
    links = jnp.where((links >= PIX + WW) & (gone_up == 0), PIX + 2 * WW, links)
    block_row = iota((32, PIX), 0)

    def build(b, carry):
        base = pl.multiple_of(b * 32, 32)
        near = links - base
        total = jnp.zeros((32, PIX), F32)
        for e in range(8):
            total = total + jnp.where(block_row == near[e : e + 1], 1.0, 0.0)
        amat[pl.ds(base, 32), :] = total.astype(BF16)
        return carry

    lax.fori_loop(0, (PIX + 2 * WW) // 32, build, 0)

    v1 = finish(0, inner(pair))
    basis[GROUP : 2 * GROUP] = v1.astype(BF16)
    pair = rim(1, v1)
    halo_start(1)
    local = inner(pair)
    exchange2(0, A1, A2)
    v2 = 2.0 * finish(1, local) - v0
    basis[2 * GROUP : 3 * GROUP] = v2.astype(BF16)
    pair = rim(2, v2)
    halo_start(2)
    local = inner(pair)
    to_pixels = jnp.where(((xcmajor - own_start) & 127) == lane, 1.0, 0.0).astype(BF16)
    columns = dot(arrived2(0, A2).astype(BF16), to_pixels).astype(BF16)
    for s in range(NCHAN):
        cs[s] = columns[s * OUT_PART : (s + 1) * OUT_PART]
    spread(CT, chan_peer, NCHAN, lambda slot: cs.at[slot], ct.at[chan])
    ct[chan] = cs[chan]
    weight = cheb[...]
    weight_t = weight.astype(F32).T.astype(BF16)
    v3 = 2.0 * finish(2, local) - v1
    basis[3 * GROUP :] = v3.astype(BF16)

    part = dot(weight_t, basis[...]).astype(BF16)
    for s in range(NCHAN):
        cp[s] = part[:, s * WW : (s + 1) * WW]
    spread(CP, chan_peer, NCHAN, lambda slot: cp.at[slot], cr.at[chan])
    cr[chan] = cp[chan]

    wg1[chan] = w1[...]
    wg2[chan] = w2[...]
    await_bytes(wg2.at[pl.ds(0, NCHAN - 1)], recv.at[W2])
    await_bytes(wg1.at[pl.ds(0, NCHAN - 1)], recv.at[W1])
    await_bytes(ct.at[pl.ds(0, NCHAN - 1)], recv.at[CT])
    cot_px = ct[...].reshape(OUTF, WW)
    cot_t = cot_px.astype(F32).T.astype(BF16)
    for h in range(NCHAN):
        dhid[h] = dot(cot_t, wg2[h], 1, 1)

    await_bytes(cr.at[pl.ds(0, NCHAN - 1)], recv.at[CP])
    total = cr[0].astype(F32)
    for s in range(1, NCHAN):
        total = total + cr[s].astype(F32)
    features = total.astype(BF16)
    features_t = total.T.astype(BF16)
    hidden, d_pre = [], []
    d_feat = jnp.zeros((WW, 128), F32)
    for h in range(NCHAN):
        pre = dot(features_t, wg1[h])
        gate = jax.nn.sigmoid(pre)
        hidden.append((pre * gate).astype(BF16))
        d_pre.append((dhid[h] * gate * (1.0 + pre * (1.0 - gate))).astype(BF16))
        d_feat = d_feat + dot(d_pre[h], wg1[h], 1, 1)
    dg_s[...] = d_feat.astype(BF16)
    spread(DG, chan_peer, NCHAN, lambda slot: dg_s, dg.at[chan])
    dg[chan] = dg_s[...]

    out_t = jnp.zeros((WW, OUTF), F32)
    for h in range(NCHAN):
        gs[h, 0:128] = dot(features, d_pre[h]).astype(BF16)
        gs[h, 128:192] = dot(cot_px, hidden[h]).astype(BF16)
        out_t = out_t + dot(hidden[h], wg2[h])
    spread(GS, chan_peer, NCHAN, lambda slot: gs.at[slot], gr.at[chan])
    gr[chan] = gs[chan]
    ms[...] = out_t.T.astype(BF16).reshape(NCHAN, OUT_PART, WW)
    spread(MO, chan_peer, NCHAN, lambda slot: ms.at[slot], mr.at[chan])
    mr[chan] = ms[chan]

    await_bytes(dg.at[pl.ds(0, NCHAN - 1)], recv.at[DG])
    d_conv_t = dg[...].reshape(PIX, 128)
    adj3 = dot(weight[3 * GROUP :], d_conv_t, 1, 1)
    pair = rim(3, adj3)
    halo_start(3)
    cheb_part = dot(basis[...], d_conv_t)
    await_bytes(gr.at[pl.ds(0, NCHAN - 1)], recv.at[GS])
    grads = gr[0].astype(F32)
    for s in range(1, NCHAN):
        grads = grads + gr[s].astype(F32)
    g1[:, 0:2] = cheb_part.reshape(NXC, 2, 8, 128)
    g1[:, 2:4] = grads[0:128].reshape(NXC, 2, 8, 128)
    g1[:, 4:5] = grads[128:192].reshape(NXC, 1, 8, 128)
    spread(G1, xc_peer, NXC, lambda slot: g1.at[slot], rg1.at[xc])
    rg1[xc] = g1[xc]
    local = inner(pair)
    d_low = dot(weight[: 3 * GROUP], d_conv_t, 1, 1)
    await_bytes(mr.at[pl.ds(0, NCHAN - 1)], recv.at[MO])
    to_rows = jnp.where(((zmajor - own_start) & 127) == lane, 1.0, 0.0).astype(BF16)
    outs = jnp.concatenate([mr[...].reshape(OUTF, WW), jnp.zeros((64, WW), BF16)], axis=0)
    exchange1(1, B1, dot(to_rows, outs, 1, 1))
    adj2 = d_low[2 * GROUP :] + 2.0 * finish(3, local)
    adj1 = d_low[GROUP : 2 * GROUP] - adj3
    pair = rim(4, adj2)
    halo_start(4)

    await_bytes(rg1.at[pl.ds(0, NXC - 1)], recv.at[G1])
    total = rg1[0]
    for s in range(1, NXC):
        total = total + rg1[s]
    hbuf[...] = total

    def to_owner(j):
        return pltpu.make_async_remote_copy(
            src_ref=hbuf.at[j], dst_ref=rg2.at[z], send_sem=g2send.at[j], recv_sem=g2recv,
            device_id=z_device(j * STRIDE), device_id_type=MESH,
        )

    for j in range(TILES):
        @pl.when(z != j * STRIDE)
        def _(j=j):
            to_owner(j).start()

        @pl.when(z == j * STRIDE)
        def _(j=j):
            rg2[z] = hbuf[j]

    local = inner(pair)
    count2, off2, first2 = places(xcmajor)
    out_row = iota((NREGION, ROWS_DEV), 1)
    for s in range(4):
        fine = (out_row == first2 + s) & (off2 + s * NREGION < count2)
        mmat[s] = jnp.where(fine, 1.0, 0.0).astype(BF16)
    adj1 = adj1 + 2.0 * finish(4, local)
    adj0 = d_low[:GROUP] - adj2
    pair = rim(5, adj1)
    halo_start(5)

    for j in range(TILES):
        @pl.when(z == j * STRIDE)
        def _(j=j):
            await_bytes(rg2.at[pl.ds(0, NZ - 1)], g2recv)
            total = rg2[0]
            for s in range(1, NZ):
                total = total + rg2[s]
            ft[...] = total
            rf[j] = total

            def step(d, carry):
                pltpu.make_async_remote_copy(
                    src_ref=ft, dst_ref=rf.at[j], send_sem=f1send, recv_sem=f1recv.at[j],
                    device_id=z_peer(d)[1], device_id_type=MESH,
                ).start()
                return carry

            lax.fori_loop(1, NZ, step, 0)

    exchange2(1, B1, B2)
    local = inner(pair)
    ig_out[...] = adj0 + finish(5, local)

    for j in range(TILES):
        @pl.when(z != j * STRIDE)
        def _(j=j):
            await_bytes(rf.at[j], f1recv.at[j])
    spread(F2, xc_peer, NXC, lambda slot: rf, fin.at[xc])
    fin[xc] = rf[...]

    rows_t = arrived2(1, B2).astype(BF16)
    result = jnp.zeros((OUT_PART, ROWS_DEV), F32)
    for s in range(4):
        result = result + dot(rows_t[s * OUT_PART : (s + 1) * OUT_PART], mmat[s])
    mo_out[...] = result.astype(BF16)

    scale = 1.0 / math.sqrt(NREGION * ROWS_DEV)
    await_bytes(fin.at[pl.ds(0, NXC - 1)], recv.at[F2])
    cg_out[...] = fin[:, 0:2].reshape(128, 128) * scale
    fg_out[...] = fin[:, 2:4].reshape(128, 128) * scale
    sg_out[...] = (fin[:, 4:5].reshape(64, 128) * scale).T

    for step in range(6):
        for side in range(2):
            halo_copy(step, side).wait_send()
    for key, ref in ((W1, wg1), (W2, wg2), (CT, ct), (CP, cr), (DG, dg), (GS, gr), (MO, mr)):
        await_bytes(ref.at[pl.ds(0, NCHAN - 1)], send.at[key])
    for k, key1, key2 in ((0, A1, A2), (1, B1, B2)):
        await_bytes(r1.at[k, pl.ds(0, NZ - 1)], send.at[key1])
        await_bytes(r2.at[k, pl.ds(0, NXC - 1)], send.at[key2])
    await_bytes(rg1.at[pl.ds(0, NXC - 1)], send.at[G1])
    await_bytes(fin.at[pl.ds(0, NXC - 1)], send.at[F2])
    for j in range(TILES):
        @pl.when(z != j * STRIDE)
        def _(j=j):
            to_owner(j).wait_send()

        @pl.when(z == j * STRIDE)
        def _():
            await_bytes(rg2.at[pl.ds(0, NZ - 1)], f1send)


def body(
    sky_maps, neighbours, send_lists, counts, cheb_weight, first_weight, second_weight, cotangent
):
    dma = pltpu.SemaphoreType.DMA
    vmem = pltpu.VMEM
    scratch = [
        vmem((PIX + 2 * WW, PIX), BF16),
        vmem((PIX, 2 * WW), BF16),
        vmem((4, NREGION, ROWS_DEV), BF16),
        vmem((ORDER * GROUP, PIX), BF16),
        vmem((6, 2, GROUP, WW), BF16),
        vmem((6, 2, GROUP, WW), BF16),
        vmem((NCHAN, 128, 128), BF16),
        vmem((NCHAN, 128, OUTF), BF16),
        vmem((2, NZ, NXC, 128), F32),
        vmem((2, NZ, NXC, 128), F32),
        vmem((2, NXC, NZ, 128), BF16),
        vmem((2, NXC, NZ, 128), BF16),
        vmem((NCHAN, OUT_PART, WW), BF16),
        vmem((NCHAN, OUT_PART, WW), BF16),
        vmem((NCHAN, 128, WW), BF16),
        vmem((NCHAN, 128, WW), BF16),
        vmem((NCHAN, WW, 128), F32),
        vmem((WW, 128), BF16),
        vmem((NCHAN, WW, 128), BF16),
        vmem((NCHAN, 192, 128), BF16),
        vmem((NCHAN, 192, 128), BF16),
        vmem((NCHAN, OUT_PART, WW), BF16),
        vmem((NCHAN, OUT_PART, WW), BF16),
        vmem((NXC, TILES, 8, 128), F32),
        vmem((NXC, TILES, 8, 128), F32),
        vmem((TILES, 8, 128), F32),
        vmem((NZ, 8, 128), F32),
        vmem((8, 128), F32),
        vmem((TILES, 8, 128), F32),
        vmem((NXC, TILES, 8, 128), F32),
        dma((6, 2)),
        dma((6, 2)),
        dma((EXCHANGES,)),
        dma((EXCHANGES,)),
        dma((TILES,)),
        dma,
        dma,
        dma((TILES,)),
    ]
    shape = jax.ShapeDtypeStruct
    mlp_out, input_grad, cheb_grad, first_grad, second_grad = pl.pallas_call(
        kernel,
        out_shape=(
            shape((OUT_PART, ROWS_DEV), BF16),
            shape((GROUP, PIX), F32),
            shape((ORDER * GROUP, 128), F32),
            shape((128, 128), F32),
            shape((128, OUTF), F32),
        ),
        in_specs=[pl.BlockSpec(memory_space=vmem)] * 8,
        out_specs=[pl.BlockSpec(memory_space=vmem)] * 5,
        scratch_shapes=scratch,
        compiler_params=pltpu.CompilerParams(
            collective_id=0, has_side_effects=True, vmem_limit_bytes=40 * 1024 * 1024
        ),
        cost_estimate=pl.CostEstimate(
            flops=600_000_000, bytes_accessed=1_000_000, transcendentals=65_536
        ),
    )(
        sky_maps,
        neighbours,
        send_lists,
        counts.reshape(1, NREGION),
        cheb_weight.reshape(ORDER * GROUP, 128),
        first_weight,
        second_weight,
        cotangent,
    )
    return mlp_out, input_grad, cheb_grad.reshape(ORDER, GROUP, 128), first_grad, second_grad


def solution(mesh):
    return jax.shard_map(
        body,
        mesh=mesh,
        in_specs=(
            P("chan", "region"),
            P(None, "region"),
            P(None, "region"),
            P(),
            P(None, "chan", None),
            P(None, "chan"),
            P("chan", None),
            P("chan", "region"),
        ),
        out_specs=(
            P("chan", "region"),
            P("chan", "region"),
            P(None, "chan", None),
            P(None, "chan"),
            P("chan", None),
        ),
        check_vma=False,
    )
```

```python
import math

import jax
import jax.numpy as jnp
from jax import lax
from jax.experimental import pallas as pl
from jax.experimental.pallas import tpu as pltpu
from jax.sharding import PartitionSpec as P

F32, BF16, I32 = jnp.float32, jnp.bfloat16, jnp.int32
MESH = pl.DeviceIdType.MESH
PIX, WW, ORDER, GROUP = 512, 128, 4, 32
NZ, NX, NXC, NCHAN, NREGION = 16, 4, 8, 4, 128
NPLANE = NXC * NCHAN
PIECE, CORE1 = 48, 32
OUT_PART, ROWS_DEV, OUTF = 16, 256, 64

W1, W2, A1, A2, CP, DG, GS, B1, B2, G1, G2, F2, EXCHANGES = range(13)


def dot(left, right, left_dim=1, right_dim=0):
    return lax.dot_general(
        left, right, (((left_dim,), (right_dim,)), ((), ())), preferred_element_type=F32
    )


def iota(shape, dim):
    return lax.broadcasted_iota(I32, shape, dim)


def kernel(
    sky_in, nb_in, sl_in, cnt_in, cheb_in, w1_in, w2_in, cot_in,
    mo_out, ig_out, cg_out, fg_out, sg_out,
    sky, nb, sl, cnt, cheb, w1, w2, cot,
    amat, smat, mmat, emat, basis, hs, hr, wg1, wg2, s1, r1, s2, r2, cp, cr, dhid,
    dg_s, dg, gs, gr, g1, rg1, hbuf, rg2, ft, fin,
    loads, hsend, hrecv, send, recv,
):
    region, chan = lax.axis_index("region"), lax.axis_index("chan")
    core, z, x = lax.rem(region, 2), lax.rem(lax.div(region, 2), NZ), lax.div(region, 2 * NZ)
    xc = x * 2 + core

    plane = xc * NCHAN + chan

    def z_peer(step):
        other = lax.rem(z + step, NZ)
        return other, ((x * NZ + other) * 2 + core, chan)

    def plane_peer(step):
        other = lax.rem(plane + step, NPLANE)
        there = lax.div(other, NCHAN)
        there = (lax.div(there, 2) * NZ + z) * 2 + lax.rem(there, 2)
        return other, (there, lax.rem(other, NCHAN))

    def xc_peer(step):
        other = lax.rem(xc + step, NXC)
        return other, ((lax.div(other, 2) * NZ + z) * 2 + lax.rem(other, 2), chan)

    def chan_peer(step):
        other = lax.rem(chan + step, NCHAN)
        return other, (region, other)

    lower = (lax.rem(region + NREGION - 1, NREGION), chan)
    upper = (lax.rem(region + 1, NREGION), chan)

    barrier = pltpu.get_barrier_semaphore()

    def greet(peer, count):
        def step(d, carry):
            pl.semaphore_signal(barrier, inc=1, device_id=peer(d)[1], device_id_type=MESH)
            return carry

        lax.fori_loop(1, count, step, 0)

    greet(z_peer, NZ)
    for device in (lower, upper):
        pl.semaphore_signal(barrier, inc=1, device_id=device, device_id_type=MESH)
    greet(plane_peer, NPLANE)

    pairs = (
        (nb_in, nb), (sl_in, sl), (sky_in, sky), (cnt_in, cnt),
        (cot_in, cot), (w1_in, w1), (w2_in, w2), (cheb_in, cheb),
    )
    load = {id(there): pltpu.make_async_copy(here, there, loads.at[i]) for i, (here, there) in enumerate(pairs)}
    for copy in load.values():
        copy.start()

    def loaded(*refs):
        for ref in refs:
            load[id(ref)].wait()

    def spread(key, peer, count, src_at, dst):
        def step(d, carry):
            slot, device = peer(d)
            pltpu.make_async_remote_copy(
                src_ref=src_at(slot), dst_ref=dst, send_sem=send.at[key],
                recv_sem=recv.at[key], device_id=device, device_id_type=MESH,
            ).start()
            return carry

        lax.fori_loop(1, count, step, 0)

    def await_bytes(ref, sem):
        pltpu.make_async_copy(ref, ref, sem).wait()

    loaded(nb, sl, sky)
    links = nb[...]
    inv = 1.0 / jnp.sqrt(
        jnp.maximum(jnp.sum((links != PIX + 2 * WW).astype(F32), axis=0, keepdims=True), 1.0)
    )
    slot_row = iota((PIX, WW), 0)
    for side in range(2):
        smat[:, side * WW : (side + 1) * WW] = (
            jnp.where(slot_row == sl[side : side + 1, :], 1.0, 0.0).astype(BF16)
        )

    def halo_copy(step, side):
        return pltpu.make_async_remote_copy(
            src_ref=hs.at[step, side], dst_ref=hr.at[step, 1 - side],
            send_sem=hsend.at[step, side], recv_sem=hrecv.at[step, 1 - side],
            device_id=(lower, upper)[side], device_id_type=MESH,
        )

    def rim(step, values):
        scaled = values * inv
        high = scaled.astype(BF16)
        edge = dot(high, smat[...]).astype(BF16)
        hs[step, 0] = edge[:, :WW]
        hs[step, 1] = edge[:, WW:]
        return scaled, high

    def halo_start(step):
        for side in range(2):
            halo_copy(step, side).start()

    def inner(pair):
        scaled, high = pair
        low = (scaled - high.astype(F32)).astype(BF16)
        both = dot(jnp.concatenate([high, low], axis=0), amat[:PIX])
        return both[:GROUP] + both[GROUP:]

    def finish(step, local):
        for side in range(2):
            halo_copy(step, 1 - side).wait_recv()
        local = local + dot(hr[step, 0], amat[PIX : PIX + WW])
        local = local + dot(hr[step, 1], amat[PIX + WW :])
        return -inv * local

    v0 = sky[...].astype(F32)
    basis[0:GROUP] = sky[...]
    pair = rim(0, v0)

    pl.semaphore_wait(barrier, 2 + (NPLANE - 1) + (NZ - 1))
    halo_start(0)

    loaded(cnt, cot)
    counts = cnt[...].astype(F32)
    own_start = jnp.sum(
        jnp.where(iota((64, NREGION), 1) < region, counts, 0.0), axis=1, keepdims=True
    )[:1].astype(I32)

    def places(order):
        lane = iota(order.shape, 1)
        count = jnp.sum(jnp.where(lane == order, counts, 0.0), axis=1, keepdims=True).astype(I32)
        start = jnp.sum(jnp.where(lane < order, counts, 0.0), axis=1, keepdims=True).astype(I32)
        off = (region - start) & (NREGION - 1)
        first = (start + off - region) >> 7
        return count, off, first

    def exchange1(k, key, message):
        s1[k] = message.reshape(NZ, NX, 128)
        spread(key, z_peer, NZ, lambda slot: s1.at[k, slot], r1.at[k, z])
        r1[k, z] = s1[k, z]

    def exchange2(k, key1, key2):
        await_bytes(r1.at[k, pl.ds(0, NZ - 1)], recv.at[key1])
        here = jnp.concatenate([r1[k, :, i, :] for i in range(NX)], axis=0).astype(BF16)
        moved = dot(here, emat[...]).astype(BF16)
        for i in range(NX):
            for b in range(2 * NCHAN):
                s2[k, i * 2 * NCHAN + b] = moved[i * NZ : (i + 1) * NZ, b * 128 : (b + 1) * 128]
        spread(key2, plane_peer, NPLANE, lambda slot: s2.at[k, slot], r2.at[k, plane])
        r2[k, plane] = s2[k, plane]

    def arrived2(k, key2):
        await_bytes(r2.at[k, pl.ds(0, NPLANE - 1)], recv.at[key2])
        parts = r2[k].astype(F32).reshape(NXC, NCHAN, NZ, 128)
        total = parts[:, 0]
        for s in range(1, NCHAN):
            total = total + parts[:, s]
        return total.reshape(NREGION, 128).T.astype(BF16)

    pair_row = iota((NZ * NX, NREGION), 0)
    zmajor = ((pair_row & 3) * NZ + (pair_row >> 2)) * 2
    count0, off0, first0 = places(zmajor)
    count1, off1, first1 = places(zmajor + 1)
    own_cot = cot[...].astype(F32)
    shifted = [own_cot] + [pltpu.roll(own_cot, ROWS_DEV - s, 1) for s in range(1, 4)]
    shifted = jnp.concatenate(shifted, axis=0).astype(BF16)
    empty = jnp.zeros_like(shifted)
    shifted = jnp.concatenate(
        [jnp.concatenate([shifted, empty], axis=1), jnp.concatenate([empty, shifted], axis=1)], axis=0
    )
    own_row = iota((NZ * NX, ROWS_DEV), 1)
    choice = jnp.concatenate([own_row == first0, own_row == first1], axis=1)
    message = dot(jnp.where(choice, 1.0, 0.0).astype(BF16), shifted, 1, 1)
    lane64 = iota((NZ * NX, NREGION), 1)
    room = jnp.where(lane64 < 64, count0 - off0, count1 - off1)
    message = jnp.where(((lane64 & 63) >> 4) * NREGION < room, message, 0.0)
    exchange1(0, A1, message)
    loaded(w1, w2)
    spread(W1, chan_peer, NCHAN, lambda slot: w1, wg1.at[chan])
    spread(W2, chan_peer, NCHAN, lambda slot: w2, wg2.at[chan])

    from_row, to_lane = iota((128, 1024), 0), iota((128, 1024), 1)
    emat[...] = jnp.where(
        ((from_row >> 4) == (to_lane >> 7))
        & ((to_lane & 127) == chan * OUT_PART + (from_row & 15)),
        1.0, 0.0,
    ).astype(BF16)

    gone = jnp.where(region == 0, 0, -1)
    gone_up = jnp.where(region == NREGION - 1, 0, -1)
    links = jnp.where((links >= PIX) & (links < PIX + WW) & (gone == 0), PIX + 2 * WW, links)
    links = jnp.where((links >= PIX + WW) & (gone_up == 0), PIX + 2 * WW, links)
    block_row = iota((32, PIX), 0)

    def build(b, carry):
        base = pl.multiple_of(b * 32, 32)
        near = links - base
        total = jnp.zeros((32, PIX), F32)
        for e in range(8):
            total = total + jnp.where(block_row == near[e : e + 1], 1.0, 0.0)
        amat[pl.ds(base, 32), :] = total.astype(BF16)
        return carry

    lax.fori_loop(0, (PIX + 2 * WW) // 32, build, 0)

    v1 = finish(0, inner(pair))
    basis[GROUP : 2 * GROUP] = v1.astype(BF16)
    pair = rim(1, v1)
    halo_start(1)
    local = inner(pair)
    v2 = 2.0 * finish(1, local) - v0
    basis[2 * GROUP : 3 * GROUP] = v2.astype(BF16)
    pair = rim(2, v2)
    halo_start(2)
    local = inner(pair)
    exchange2(0, A1, A2)
    lane, row = iota((NREGION, NREGION), 1), iota((NREGION, NREGION), 0)
    xcmajor = (((row >> 5) * NZ + (row & 15)) * 2) + ((row >> 4) & 1)
    to_pixels = jnp.where(((xcmajor - own_start) & 127) == lane, 1.0, 0.0).astype(BF16)
    loaded(cheb)
    weight = cheb[...]
    weight_t = weight.astype(F32).T.astype(BF16)
    v3 = 2.0 * finish(2, local) - v1
    basis[3 * GROUP :] = v3.astype(BF16)

    part = dot(weight_t, basis[...]).astype(BF16)
    for s in range(NCHAN):
        cp[s] = part[:, s * WW : (s + 1) * WW]
    spread(CP, chan_peer, NCHAN, lambda slot: cp.at[slot], cr.at[chan])
    cr[chan] = cp[chan]

    wg1[chan] = w1[...]
    wg2[chan] = w2[...]
    await_bytes(wg2.at[pl.ds(0, NCHAN - 1)], recv.at[W2])
    await_bytes(wg1.at[pl.ds(0, NCHAN - 1)], recv.at[W1])
    columns = dot(arrived2(0, A2), to_pixels)[:OUTF]
    cot_px = columns.astype(BF16)
    cot_t = columns.T.astype(BF16)
    for h in range(NCHAN):
        dhid[h] = dot(cot_t, wg2[h])

    await_bytes(cr.at[pl.ds(0, NCHAN - 1)], recv.at[CP])
    total = cr[0].astype(F32)
    for s in range(1, NCHAN):
        total = total + cr[s].astype(F32)
    features = total.astype(BF16)
    features_t = total.T.astype(BF16)
    hidden, d_pre = [], []
    d_feat = jnp.zeros((WW, 128), F32)
    for h in range(NCHAN):
        pre = dot(features_t, wg1[h])
        gate = jax.nn.sigmoid(pre)
        hidden.append((pre * gate).astype(BF16))
        d_pre.append((dhid[h] * gate * (1.0 + pre * (1.0 - gate))).astype(BF16))
        d_feat = d_feat + dot(d_pre[h], wg1[h], 1, 1)
    dg_s[...] = d_feat.astype(BF16)
    spread(DG, chan_peer, NCHAN, lambda slot: dg_s, dg.at[chan])
    dg[chan] = dg_s[...]

    out_t = jnp.zeros((WW, OUTF), F32)
    for h in range(NCHAN):
        gs[h, 0:128] = dot(features, d_pre[h]).astype(BF16)
        gs[h, 128:192] = dot(cot_px, hidden[h]).astype(BF16)
        out_t = out_t + dot(hidden[h], wg2[h], 1, 1)
    spread(GS, chan_peer, NCHAN, lambda slot: gs.at[slot], gr.at[chan])
    gr[chan] = gs[chan]
    outs = out_t.T.astype(BF16)
    empty = jnp.zeros_like(outs)
    outs = jnp.concatenate(
        [jnp.concatenate([outs, empty], axis=1), jnp.concatenate([empty, outs], axis=1)], axis=0
    )
    to_rows = jnp.concatenate(
        [((zmajor + i - own_start) & 127) == lane64 for i in range(2)], axis=1
    )
    exchange1(1, B1, dot(jnp.where(to_rows, 1.0, 0.0).astype(BF16), outs, 1, 1))

    await_bytes(dg.at[pl.ds(0, NCHAN - 1)], recv.at[DG])
    d_conv_t = dg[...].reshape(PIX, 128)
    adj3 = dot(weight[3 * GROUP :], d_conv_t, 1, 1)
    pair = rim(3, adj3)
    halo_start(3)
    cheb_part = dot(basis[...], d_conv_t)
    await_bytes(gr.at[pl.ds(0, NCHAN - 1)], recv.at[GS])
    grads = gr[0].astype(F32)
    for s in range(1, NCHAN):
        grads = grads + gr[s].astype(F32)
    g1[:, 0:16] = cheb_part.astype(BF16).reshape(NXC, 16, 128)
    g1[:, 16:32] = grads[0:128].astype(BF16).reshape(NXC, 16, 128)
    for i in range(NX):
        g1[2 * i, 32:48] = grads[128 + 16 * i : 144 + 16 * i].astype(BF16)
        g1[2 * i + 1, 32:48] = jnp.zeros((16, 128), BF16)
    spread(G1, xc_peer, NXC, lambda slot: g1.at[slot], rg1.at[xc])
    rg1[xc] = g1[xc]
    local = inner(pair)
    d_low = dot(weight[: 3 * GROUP], d_conv_t, 1, 1)
    adj2 = d_low[2 * GROUP :] + 2.0 * finish(3, local)
    adj1 = d_low[GROUP : 2 * GROUP] - adj3
    pair = rim(4, adj2)
    halo_start(4)

    await_bytes(rg1.at[pl.ds(0, NXC - 1)], recv.at[G1])
    total = rg1[0].astype(F32)
    for s in range(1, NXC):
        total = total + rg1[s].astype(F32)
    hbuf[...] = total.astype(BF16)
    for own_core, rows in ((0, PIECE), (1, CORE1)):
        @pl.when(core == own_core)
        def _(rows=rows):
            spread(G2, z_peer, NZ, lambda slot: hbuf.at[pl.ds(0, rows)], rg2.at[z, pl.ds(0, rows)])

    rg2[z] = hbuf[...]
    exchange2(1, B1, B2)
    local = inner(pair)
    count2, off2, first2 = places(xcmajor)
    out_row = iota((NREGION, ROWS_DEV), 1)
    for s in range(4):
        fine = (out_row == first2 + s) & (off2 + s * NREGION < count2)
        mmat[s] = jnp.where(fine, 1.0, 0.0).astype(BF16)
    adj1 = adj1 + 2.0 * finish(4, local)
    adj0 = d_low[:GROUP] - adj2
    pair = rim(5, adj1)
    halo_start(5)

    local = inner(pair)
    ig_out[...] = adj0 + finish(5, local)

    for own_core, rows in ((0, PIECE), (1, CORE1)):
        @pl.when(core == own_core)
        def _(rows=rows):
            await_bytes(rg2.at[pl.ds(0, NZ - 1), pl.ds(0, rows)], recv.at[G2])
            total = rg2[0, 0:rows].astype(F32)
            for s in range(1, NZ):
                total = total + rg2[s, 0:rows].astype(F32)
            ft[0:rows] = total.astype(BF16)
            if rows < PIECE:
                ft[rows:] = jnp.zeros((PIECE - rows, 128), BF16)

    spread(F2, xc_peer, NXC, lambda slot: ft, fin.at[xc])
    fin[xc] = ft[...]

    rows_t = arrived2(1, B2)
    result = jnp.zeros((OUT_PART, ROWS_DEV), F32)
    for s in range(4):
        result = result + dot(rows_t[s * OUT_PART : (s + 1) * OUT_PART], mmat[s])
    mo_out[...] = result.astype(BF16)

    scale = 1.0 / math.sqrt(NREGION * ROWS_DEV)
    await_bytes(fin.at[pl.ds(0, NXC - 1)], recv.at[F2])
    cg_out[...] = fin[:, 0:16].astype(F32).reshape(128, 128) * scale
    fg_out[...] = fin[:, 16:32].astype(F32).reshape(128, 128) * scale
    for i in range(NX):
        sg_out[16 * i : 16 * (i + 1)] = fin[2 * i, 32:48].astype(F32) * scale

    for step in range(6):
        for side in range(2):
            halo_copy(step, side).wait_send()
    for key, ref in ((W1, wg1), (W2, wg2), (CP, cr), (DG, dg), (GS, gr)):
        await_bytes(ref.at[pl.ds(0, NCHAN - 1)], send.at[key])
    for k, key1, key2 in ((0, A1, A2), (1, B1, B2)):
        await_bytes(r1.at[k, pl.ds(0, NZ - 1)], send.at[key1])
        await_bytes(r2.at[k, pl.ds(0, NPLANE - 1)], send.at[key2])
    await_bytes(rg1.at[pl.ds(0, NXC - 1)], send.at[G1])
    await_bytes(fin.at[pl.ds(0, NXC - 1)], send.at[F2])
    for own_core, rows in ((0, PIECE), (1, CORE1)):
        @pl.when(core == own_core)
        def _(rows=rows):
            await_bytes(rg2.at[pl.ds(0, NZ - 1), pl.ds(0, rows)], send.at[G2])


def writer(*refs):
    count = len(refs) // 2
    sems = refs[-1]
    copies = [pltpu.make_async_copy(refs[i], refs[count + i], sems.at[i]) for i in range(count)]
    for copy in copies:
        copy.start()
    for copy in copies:
        copy.wait()


def body(
    sky_maps, neighbours, send_lists, counts, cheb_weight, first_weight, second_weight, cotangent
):
    dma = pltpu.SemaphoreType.DMA
    vmem = pltpu.VMEM
    shape = jax.ShapeDtypeStruct
    args = (
        sky_maps,
        neighbours,
        send_lists,
        counts.reshape(1, NREGION),
        cheb_weight.reshape(ORDER * GROUP, 128),
        first_weight,
        second_weight.T,
        cotangent,
    )
    scratch = [vmem(arg.shape, arg.dtype) for arg in args] + [
        vmem((PIX + 2 * WW, PIX), BF16),
        vmem((PIX, 2 * WW), BF16),
        vmem((4, NREGION, ROWS_DEV), BF16),
        vmem((128, 1024), BF16),
        vmem((ORDER * GROUP, PIX), BF16),
        vmem((6, 2, GROUP, WW), BF16),
        vmem((6, 2, GROUP, WW), BF16),
        vmem((NCHAN, 128, 128), BF16),
        vmem((NCHAN, OUTF, 128), BF16),
        vmem((2, NZ, NX, 128), F32),
        vmem((2, NZ, NX, 128), F32),
        vmem((2, NPLANE, NZ, 128), BF16),
        vmem((2, NPLANE, NZ, 128), BF16),
        vmem((NCHAN, 128, WW), BF16),
        vmem((NCHAN, 128, WW), BF16),
        vmem((NCHAN, WW, 128), F32),
        vmem((WW, 128), BF16),
        vmem((NCHAN, WW, 128), BF16),
        vmem((NCHAN, 192, 128), BF16),
        vmem((NCHAN, 192, 128), BF16),
        vmem((NXC, PIECE, 128), BF16),
        vmem((NXC, PIECE, 128), BF16),
        vmem((PIECE, 128), BF16),
        vmem((NZ, PIECE, 128), BF16),
        vmem((PIECE, 128), BF16),
        vmem((NXC, PIECE, 128), BF16),
        dma((8,)),
        dma((6, 2)),
        dma((6, 2)),
        dma((EXCHANGES,)),
        dma((EXCHANGES,)),
    ]
    results = (
        shape((OUT_PART, ROWS_DEV), BF16),
        shape((GROUP, PIX), F32),
        shape((ORDER * GROUP, 128), F32),
        shape((128, 128), F32),
        shape((OUTF, 128), F32),
    )
    found = pl.pallas_call(
        kernel,
        out_shape=results,
        in_specs=[pl.BlockSpec(memory_space=pl.ANY)] * 8,
        out_specs=[pl.BlockSpec(memory_space=vmem)] * 5,
        scratch_shapes=scratch,
        compiler_params=pltpu.CompilerParams(
            collective_id=0, has_side_effects=True, vmem_limit_bytes=60 * 1024 * 1024
        ),
        cost_estimate=pl.CostEstimate(
            flops=600_000_000, bytes_accessed=1_000_000, transcendentals=65_536
        ),
    )(*args)
    mlp_out, input_grad, cheb_grad, first_grad, second_grad = pl.pallas_call(
        writer,
        out_shape=results,
        in_specs=[pl.BlockSpec(memory_space=pl.ANY)] * 5,
        out_specs=[pl.BlockSpec(memory_space=pl.ANY)] * 5,
        scratch_shapes=[dma((5,))],
    )(*found)
    return mlp_out, input_grad, cheb_grad.reshape(ORDER, GROUP, 128), first_grad, second_grad.T


def solution(mesh):
    return jax.shard_map(
        body,
        mesh=mesh,
        in_specs=(
            P("chan", "region"),
            P(None, "region"),
            P(None, "region"),
            P(),
            P(None, "chan", None),
            P(None, "chan"),
            P("chan", None),
            P("chan", "region"),
        ),
        out_specs=(
            P("chan", "region"),
            P("chan", "region"),
            P(None, "chan", None),
            P(None, "chan"),
            P("chan", None),
        ),
        check_vma=False,
    )
```

```python
import math

import jax
import jax.numpy as jnp
from jax import lax
from jax.experimental import pallas as pl
from jax.experimental.pallas import tpu as pltpu
from jax.sharding import PartitionSpec as P

F32, BF16, I32 = jnp.float32, jnp.bfloat16, jnp.int32
MESH = pl.DeviceIdType.MESH
PIX, WW, ORDER, GROUP = 512, 128, 4, 32
NZ, NX, NXC, NCHAN, NREGION = 16, 4, 8, 4, 128
NPLANE = NXC * NCHAN
NDUO, TILE = 16, 16
OUT_PART, ROWS_DEV, OUTF = 16, 256, 64

W1, W2, A1, A2, CP, DG, GS, B1, B2, G1, G2, F2, H1, H2, I2, EXCHANGES = range(16)


def dot(left, right, left_dim=1, right_dim=0):
    return lax.dot_general(
        left, right, (((left_dim,), (right_dim,)), ((), ())), preferred_element_type=F32
    )


def iota(shape, dim):
    return lax.broadcasted_iota(I32, shape, dim)


def kernel(
    sky_in, nb_in, sl_in, cnt_in, cheb_in, w1_in, w2_in, cot_in,
    mo_out, ig_out, cg_out, fg_out, sg_out,
    sky, nb, sl, cnt, cheb, w1, w2, cot,
    amat, smat, mmat, emat, basis, hs, hr, wg1, wg2, s1, r1, s2, r2, cp, cr, dhid,
    dg_s, dg, gs, gr, g1, rg1, g2, rg2, ft, fin, h1, rh1, h2, rh2, fs, fins,
    loads, hsend, hrecv, send, recv, h1send,
):
    region, chan = lax.axis_index("region"), lax.axis_index("chan")
    core, z, x = lax.rem(region, 2), lax.rem(lax.div(region, 2), NZ), lax.div(region, 2 * NZ)
    xc = x * 2 + core

    plane = xc * NCHAN + chan

    def z_peer(step):
        other = lax.rem(z + step, NZ)
        return other, ((x * NZ + other) * 2 + core, chan)

    def plane_peer(step):
        other = lax.rem(plane + step, NPLANE)
        there = lax.div(other, NCHAN)
        there = (lax.div(there, 2) * NZ + z) * 2 + lax.rem(there, 2)
        return other, (there, lax.rem(other, NCHAN))

    parity, z_pair = lax.rem(z, 2), lax.div(z, 2)
    duo = xc * 2 + parity
    holder = duo == x * 4

    def duo_device(other):
        there = lax.div(other, 4) * NZ + z_pair * 2 + lax.rem(other, 2)
        return there * 2 + lax.rem(lax.div(other, 2), 2), chan

    def duo_peer(step):
        other = lax.rem(duo + step, NDUO)
        return other, duo_device(other)

    def line_peer(step):
        other = lax.rem(z_pair + step, NZ // 2)
        return other, ((x * NZ + other * 2 + parity) * 2 + core, chan)

    def chan_peer(step):
        other = lax.rem(chan + step, NCHAN)
        return other, (region, other)

    lower = (lax.rem(region + NREGION - 1, NREGION), chan)
    upper = (lax.rem(region + 1, NREGION), chan)

    barrier = pltpu.get_barrier_semaphore()

    def greet(peer, count):
        def step(d, carry):
            pl.semaphore_signal(barrier, inc=1, device_id=peer(d)[1], device_id_type=MESH)
            return carry

        lax.fori_loop(1, count, step, 0)

    greet(z_peer, NZ)
    for device in (lower, upper):
        pl.semaphore_signal(barrier, inc=1, device_id=device, device_id_type=MESH)
    greet(duo_peer, NDUO)
    greet(plane_peer, NPLANE)

    pairs = (
        (nb_in, nb), (sl_in, sl), (sky_in, sky), (cnt_in, cnt),
        (cot_in, cot), (w1_in, w1), (w2_in, w2), (cheb_in, cheb),
    )
    load = {id(there): pltpu.make_async_copy(here, there, loads.at[i]) for i, (here, there) in enumerate(pairs)}
    for copy in load.values():
        copy.start()

    def loaded(*refs):
        for ref in refs:
            load[id(ref)].wait()

    def spread(key, peer, count, src_at, dst):
        def step(d, carry):
            slot, device = peer(d)
            pltpu.make_async_remote_copy(
                src_ref=src_at(slot), dst_ref=dst, send_sem=send.at[key],
                recv_sem=recv.at[key], device_id=device, device_id_type=MESH,
            ).start()
            return carry

        lax.fori_loop(1, count, step, 0)

    def await_bytes(ref, sem):
        pltpu.make_async_copy(ref, ref, sem).wait()

    loaded(nb, sl, sky)
    links = nb[...]
    inv = 1.0 / jnp.sqrt(
        jnp.maximum(jnp.sum((links != PIX + 2 * WW).astype(F32), axis=0, keepdims=True), 1.0)
    )
    slot_row = iota((PIX, WW), 0)
    for side in range(2):
        smat[:, side * WW : (side + 1) * WW] = (
            jnp.where(slot_row == sl[side : side + 1, :], 1.0, 0.0).astype(BF16)
        )

    def halo_copy(step, side):
        return pltpu.make_async_remote_copy(
            src_ref=hs.at[step, side], dst_ref=hr.at[step, 1 - side],
            send_sem=hsend.at[step, side], recv_sem=hrecv.at[step, 1 - side],
            device_id=(lower, upper)[side], device_id_type=MESH,
        )

    def rim(step, values):
        scaled = values * inv
        high = scaled.astype(BF16)
        edge = dot(high, smat[...]).astype(BF16)
        hs[step, 0] = edge[:, :WW]
        hs[step, 1] = edge[:, WW:]
        return scaled, high

    def halo_start(step):
        for side in range(2):
            halo_copy(step, side).start()

    def inner(pair):
        scaled, high = pair
        low = (scaled - high.astype(F32)).astype(BF16)
        both = dot(jnp.concatenate([high, low], axis=0), amat[:PIX])
        return both[:GROUP] + both[GROUP:]

    def finish(step, local):
        for side in range(2):
            halo_copy(step, 1 - side).wait_recv()
        local = local + dot(hr[step, 0], amat[PIX : PIX + WW])
        local = local + dot(hr[step, 1], amat[PIX + WW :])
        return -inv * local

    v0 = sky[...].astype(F32)
    basis[0:GROUP] = sky[...]
    pair = rim(0, v0)

    loaded(cnt, cot)
    counts = cnt[...].astype(F32)
    own_start = jnp.sum(
        jnp.where(iota((64, NREGION), 1) < region, counts, 0.0), axis=1, keepdims=True
    )[:1].astype(I32)

    def places(order):
        lane = iota(order.shape, 1)
        count = jnp.sum(jnp.where(lane == order, counts, 0.0), axis=1, keepdims=True).astype(I32)
        start = jnp.sum(jnp.where(lane < order, counts, 0.0), axis=1, keepdims=True).astype(I32)
        off = (region - start) & (NREGION - 1)
        first = (start + off - region) >> 7
        return count, off, first

    def exchange1(k, message):
        s1[k] = message.reshape(NZ, NX, 128)

    def exchange1_start(k, key):
        spread(key, z_peer, NZ, lambda slot: s1.at[k, slot], r1.at[k, z])
        r1[k, z] = s1[k, z]

    def exchange2(k, key1, key2):
        await_bytes(r1.at[k, pl.ds(0, NZ - 1)], recv.at[key1])
        here = jnp.concatenate([r1[k, :, i, :] for i in range(NX)], axis=0).astype(BF16)
        moved = dot(here, emat[...]).astype(BF16)
        for i in range(NX):
            for b in range(2 * NCHAN):
                s2[k, i * 2 * NCHAN + b] = moved[i * NZ : (i + 1) * NZ, b * 128 : (b + 1) * 128]
        spread(key2, plane_peer, NPLANE, lambda slot: s2.at[k, slot], r2.at[k, plane])
        r2[k, plane] = s2[k, plane]

    def arrived2(k, key2):
        await_bytes(r2.at[k, pl.ds(0, NPLANE - 1)], recv.at[key2])
        parts = r2[k].astype(F32).reshape(NXC, NCHAN, NZ, 128)
        total = parts[:, 0]
        for s in range(1, NCHAN):
            total = total + parts[:, s]
        return total.reshape(NREGION, 128).T.astype(BF16)

    pair_row = iota((NZ * NX, NREGION), 0)
    zmajor = ((pair_row & 3) * NZ + (pair_row >> 2)) * 2
    count0, off0, first0 = places(zmajor)
    count1, off1, first1 = places(zmajor + 1)
    own_cot = cot[...].astype(F32)
    shifted = [own_cot] + [pltpu.roll(own_cot, ROWS_DEV - s, 1) for s in range(1, 4)]
    shifted = jnp.concatenate(shifted, axis=0).astype(BF16)
    empty = jnp.zeros_like(shifted)
    shifted = jnp.concatenate(
        [jnp.concatenate([shifted, empty], axis=1), jnp.concatenate([empty, shifted], axis=1)], axis=0
    )
    own_row = iota((NZ * NX, ROWS_DEV), 1)
    choice = jnp.concatenate([own_row == first0, own_row == first1], axis=1)
    message = dot(jnp.where(choice, 1.0, 0.0).astype(BF16), shifted, 1, 1)
    lane64 = iota((NZ * NX, NREGION), 1)
    room = jnp.where(lane64 < 64, count0 - off0, count1 - off1)
    message = jnp.where(((lane64 & 63) >> 4) * NREGION < room, message, 0.0)
    exchange1(0, message)
    gone = jnp.where(region == 0, 0, -1)
    gone_up = jnp.where(region == NREGION - 1, 0, -1)
    links = jnp.where((links >= PIX) & (links < PIX + WW) & (gone == 0), PIX + 2 * WW, links)
    links = jnp.where((links >= PIX + WW) & (gone_up == 0), PIX + 2 * WW, links)
    block_row = iota((32, PIX), 0)

    def build(b, carry):
        base = pl.multiple_of(b * 32, 32)
        near = links - base
        total = jnp.zeros((32, PIX), F32)
        for e in range(8):
            total = total + jnp.where(block_row == near[e : e + 1], 1.0, 0.0)
        amat[pl.ds(base, 32), :] = total.astype(BF16)
        return carry

    lax.fori_loop(0, (PIX + 2 * WW) // 32, build, 0)

    pl.semaphore_wait(barrier, 2 + (NPLANE - 1) + (NZ - 1) + (NDUO - 1))
    halo_start(0)

    exchange1_start(0, A1)
    loaded(w1, w2)
    spread(W1, chan_peer, NCHAN, lambda slot: w1, wg1.at[chan])
    spread(W2, chan_peer, NCHAN, lambda slot: w2, wg2.at[chan])

    local = inner(pair)
    from_row, to_lane = iota((128, 1024), 0), iota((128, 1024), 1)
    emat[...] = jnp.where(
        ((from_row >> 4) == (to_lane >> 7))
        & ((to_lane & 127) == chan * OUT_PART + (from_row & 15)),
        1.0, 0.0,
    ).astype(BF16)
    lane, row = iota((NREGION, NREGION), 1), iota((NREGION, NREGION), 0)
    xcmajor = (((row >> 5) * NZ + (row & 15)) * 2) + ((row >> 4) & 1)
    to_pixels = jnp.where(((xcmajor - own_start) & 127) == lane, 1.0, 0.0).astype(BF16)
    to_rows = jnp.concatenate(
        [((zmajor + i - own_start) & 127) == lane64 for i in range(2)], axis=1
    )
    to_rows = jnp.where(to_rows, 1.0, 0.0).astype(BF16)
    loaded(cheb)
    weight = cheb[...]
    weight_t = weight.astype(F32).T.astype(BF16)
    v1 = finish(0, local)
    basis[GROUP : 2 * GROUP] = v1.astype(BF16)
    pair = rim(1, v1)
    halo_start(1)
    local = inner(pair)
    v2 = 2.0 * finish(1, local) - v0
    basis[2 * GROUP : 3 * GROUP] = v2.astype(BF16)
    pair = rim(2, v2)
    halo_start(2)
    local = inner(pair)
    exchange2(0, A1, A2)
    v3 = 2.0 * finish(2, local) - v1
    basis[3 * GROUP :] = v3.astype(BF16)

    part = dot(weight_t, basis[...]).astype(BF16)
    for s in range(NCHAN):
        cp[s] = part[:, s * WW : (s + 1) * WW]
    spread(CP, chan_peer, NCHAN, lambda slot: cp.at[slot], cr.at[chan])
    cr[chan] = cp[chan]

    wg1[chan] = w1[...]
    wg2[chan] = w2[...]
    await_bytes(wg2.at[pl.ds(0, NCHAN - 1)], recv.at[W2])
    await_bytes(wg1.at[pl.ds(0, NCHAN - 1)], recv.at[W1])
    columns = dot(arrived2(0, A2), to_pixels)[:OUTF]
    cot_px = columns.astype(BF16)
    cot_t = columns.T.astype(BF16)
    for h in range(NCHAN):
        dhid[h] = dot(cot_t, wg2[h])

    await_bytes(cr.at[pl.ds(0, NCHAN - 1)], recv.at[CP])
    total = cr[0].astype(F32)
    for s in range(1, NCHAN):
        total = total + cr[s].astype(F32)
    features = total.astype(BF16)
    features_t = total.T.astype(BF16)
    hidden, d_pre = [], []
    d_feat = jnp.zeros((WW, 128), F32)
    for h in range(NCHAN):
        pre = dot(features_t, wg1[h])
        gate = jax.nn.sigmoid(pre)
        hidden.append((pre * gate).astype(BF16))
        d_pre.append((dhid[h] * gate * (1.0 + pre * (1.0 - gate))).astype(BF16))
        d_feat = d_feat + dot(d_pre[h], wg1[h], 1, 1)
    dg_s[...] = d_feat.astype(BF16)
    spread(DG, chan_peer, NCHAN, lambda slot: dg_s, dg.at[chan])
    dg[chan] = dg_s[...]

    out_t = jnp.zeros((WW, OUTF), F32)
    for h in range(NCHAN):
        gs[h, 0:128] = dot(features, d_pre[h]).astype(BF16)
        gs[h, 128:192] = dot(cot_px, hidden[h]).astype(BF16)
        out_t = out_t + dot(hidden[h], wg2[h], 1, 1)
    spread(GS, chan_peer, NCHAN, lambda slot: gs.at[slot], gr.at[chan])
    gr[chan] = gs[chan]
    outs = out_t.T.astype(BF16)
    empty = jnp.zeros_like(outs)
    outs = jnp.concatenate(
        [jnp.concatenate([outs, empty], axis=1), jnp.concatenate([empty, outs], axis=1)], axis=0
    )
    exchange1(1, dot(to_rows, outs, 1, 1))
    exchange1_start(1, B1)

    await_bytes(dg.at[pl.ds(0, NCHAN - 1)], recv.at[DG])
    d_conv_t = dg[...].reshape(PIX, 128)
    adj3 = dot(weight[3 * GROUP :], d_conv_t, 1, 1)
    pair = rim(3, adj3)
    halo_start(3)
    cheb_part = dot(basis[...], d_conv_t)
    await_bytes(gr.at[pl.ds(0, NCHAN - 1)], recv.at[GS])
    grads = gr[0].astype(F32)
    for s in range(1, NCHAN):
        grads = grads + gr[s].astype(F32)
    for i in range(NXC):
        g1[2 * i] = cheb_part[TILE * i : TILE * (i + 1)].astype(BF16)
        g1[2 * i + 1] = grads[TILE * i : TILE * (i + 1)].astype(BF16)
    for i in range(NX):
        h1[i] = grads[128 + TILE * i : 128 + TILE * (i + 1)].astype(BF16)
    spread(G1, duo_peer, NDUO, lambda slot: g1.at[slot], rg1.at[duo])

    def to_holder(i):
        return pltpu.make_async_remote_copy(
            src_ref=h1.at[i], dst_ref=rh1.at[duo], send_sem=h1send.at[i], recv_sem=recv.at[H1],
            device_id=duo_device(4 * i), device_id_type=MESH,
        )

    for i in range(NX):
        @pl.when(duo != 4 * i)
        def _(i=i):
            to_holder(i).start()

        @pl.when(duo == 4 * i)
        def _(i=i):
            rh1[duo] = h1[i]

    rg1[duo] = g1[duo]
    local = inner(pair)
    d_low = dot(weight[: 3 * GROUP], d_conv_t, 1, 1)
    adj2 = d_low[2 * GROUP :] + 2.0 * finish(3, local)
    adj1 = d_low[GROUP : 2 * GROUP] - adj3
    pair = rim(4, adj2)
    halo_start(4)

    def sum_of(ref, count):
        total = ref[0].astype(F32)
        for s in range(1, count):
            total = total + ref[s].astype(F32)
        return total.astype(BF16)

    await_bytes(rg1.at[pl.ds(0, NDUO - 1)], recv.at[G1])
    g2[...] = sum_of(rg1, NDUO)
    spread(G2, line_peer, NZ // 2, lambda slot: g2, rg2.at[z_pair])
    rg2[z_pair] = g2[...]

    @pl.when(holder)
    def _():
        await_bytes(rh1.at[pl.ds(0, NDUO - 1)], recv.at[H1])
        h2[...] = sum_of(rh1, NDUO)
        spread(H2, line_peer, NZ // 2, lambda slot: h2, rh2.at[z_pair])
        rh2[z_pair] = h2[...]

    exchange2(1, B1, B2)
    local = inner(pair)
    count2, off2, first2 = places(xcmajor)
    out_row = iota((NREGION, ROWS_DEV), 1)
    for s in range(4):
        fine = (out_row == first2 + s) & (off2 + s * NREGION < count2)
        mmat[s] = jnp.where(fine, 1.0, 0.0).astype(BF16)
    adj1 = adj1 + 2.0 * finish(4, local)
    adj0 = d_low[:GROUP] - adj2
    pair = rim(5, adj1)
    halo_start(5)

    local = inner(pair)
    ig_out[...] = adj0 + finish(5, local)

    rows_t = arrived2(1, B2)
    result = jnp.zeros((OUT_PART, ROWS_DEV), F32)
    for s in range(4):
        result = result + dot(rows_t[s * OUT_PART : (s + 1) * OUT_PART], mmat[s])
    mo_out[...] = result.astype(BF16)

    await_bytes(rg2.at[pl.ds(0, NZ // 2 - 1)], recv.at[G2])
    ft[...] = sum_of(rg2, NZ // 2)
    spread(F2, duo_peer, NDUO, lambda slot: ft, fin.at[duo])
    fin[duo] = ft[...]

    @pl.when(holder)
    def _():
        await_bytes(rh2.at[pl.ds(0, NZ // 2 - 1)], recv.at[H2])
        fs[...] = sum_of(rh2, NZ // 2)
        spread(I2, duo_peer, NDUO, lambda slot: fs, fins.at[x])
        fins[x] = fs[...]
        await_bytes(fins.at[pl.ds(0, NX - 1)], recv.at[I2])

    @pl.when(jnp.logical_not(holder))
    def _():
        await_bytes(fins, recv.at[I2])

    scale = 1.0 / math.sqrt(NREGION * ROWS_DEV)
    await_bytes(fin.at[pl.ds(0, NDUO - 1)], recv.at[F2])
    for i in range(NXC):
        cg_out[TILE * i : TILE * (i + 1)] = fin[2 * i].astype(F32) * scale
        fg_out[TILE * i : TILE * (i + 1)] = fin[2 * i + 1].astype(F32) * scale
    sg_out[...] = fins[...].astype(F32).reshape(OUTF, 128) * scale

    for step in range(6):
        for side in range(2):
            halo_copy(step, side).wait_send()
    for key, ref in ((W1, wg1), (W2, wg2), (CP, cr), (DG, dg), (GS, gr)):
        await_bytes(ref.at[pl.ds(0, NCHAN - 1)], send.at[key])
    for k, key1, key2 in ((0, A1, A2), (1, B1, B2)):
        await_bytes(r1.at[k, pl.ds(0, NZ - 1)], send.at[key1])
        await_bytes(r2.at[k, pl.ds(0, NPLANE - 1)], send.at[key2])
    await_bytes(rg1.at[pl.ds(0, NDUO - 1)], send.at[G1])
    await_bytes(rg2.at[pl.ds(0, NZ // 2 - 1)], send.at[G2])
    await_bytes(fin.at[pl.ds(0, NDUO - 1)], send.at[F2])
    for i in range(NX):
        @pl.when(duo != 4 * i)
        def _(i=i):
            to_holder(i).wait_send()

    @pl.when(holder)
    def _():
        await_bytes(rh2.at[pl.ds(0, NZ // 2 - 1)], send.at[H2])
        await_bytes(rh1.at[pl.ds(0, NDUO - 1)], send.at[I2])


def writer(*refs):
    count = len(refs) // 2
    for i in range(count):
        refs[count + i][...] = refs[i][...]


def body(
    sky_maps, neighbours, send_lists, counts, cheb_weight, first_weight, second_weight, cotangent
):
    dma = pltpu.SemaphoreType.DMA
    vmem = pltpu.VMEM
    shape = jax.ShapeDtypeStruct
    args = (
        sky_maps,
        neighbours,
        send_lists,
        counts.reshape(1, NREGION),
        cheb_weight.reshape(ORDER * GROUP, 128),
        first_weight,
        second_weight.T,
        cotangent,
    )
    scratch = [vmem(arg.shape, arg.dtype) for arg in args] + [
        vmem((PIX + 2 * WW, PIX), BF16),
        vmem((PIX, 2 * WW), BF16),
        vmem((4, NREGION, ROWS_DEV), BF16),
        vmem((128, 1024), BF16),
        vmem((ORDER * GROUP, PIX), BF16),
        vmem((6, 2, GROUP, WW), BF16),
        vmem((6, 2, GROUP, WW), BF16),
        vmem((NCHAN, 128, 128), BF16),
        vmem((NCHAN, OUTF, 128), BF16),
        vmem((2, NZ, NX, 128), F32),
        vmem((2, NZ, NX, 128), F32),
        vmem((2, NPLANE, NZ, 128), BF16),
        vmem((2, NPLANE, NZ, 128), BF16),
        vmem((NCHAN, 128, WW), BF16),
        vmem((NCHAN, 128, WW), BF16),
        vmem((NCHAN, WW, 128), F32),
        vmem((WW, 128), BF16),
        vmem((NCHAN, WW, 128), BF16),
        vmem((NCHAN, 192, 128), BF16),
        vmem((NCHAN, 192, 128), BF16),
        vmem((NDUO, TILE, 128), BF16),
        vmem((NDUO, TILE, 128), BF16),
        vmem((TILE, 128), BF16),
        vmem((NZ // 2, TILE, 128), BF16),
        vmem((TILE, 128), BF16),
        vmem((NDUO, TILE, 128), BF16),
        vmem((NX, TILE, 128), BF16),
        vmem((NDUO, TILE, 128), BF16),
        vmem((TILE, 128), BF16),
        vmem((NZ // 2, TILE, 128), BF16),
        vmem((TILE, 128), BF16),
        vmem((NX, TILE, 128), BF16),
        dma((8,)),
        dma((6, 2)),
        dma((6, 2)),
        dma((EXCHANGES,)),
        dma((EXCHANGES,)),
        dma((NX,)),
    ]
    results = (
        shape((OUT_PART, ROWS_DEV), BF16),
        shape((GROUP, PIX), F32),
        shape((ORDER * GROUP, 128), F32),
        shape((128, 128), F32),
        shape((OUTF, 128), F32),
    )
    found = pl.pallas_call(
        kernel,
        out_shape=results,
        in_specs=[pl.BlockSpec(memory_space=pl.ANY)] * 8,
        out_specs=[pl.BlockSpec(memory_space=vmem)] * 5,
        scratch_shapes=scratch,
        compiler_params=pltpu.CompilerParams(
            collective_id=0, has_side_effects=True, vmem_limit_bytes=60 * 1024 * 1024
        ),
        cost_estimate=pl.CostEstimate(
            flops=600_000_000, bytes_accessed=1_000_000, transcendentals=65_536
        ),
    )(*args)
    mlp_out, input_grad, cheb_grad, first_grad, second_grad = pl.pallas_call(
        writer,
        out_shape=results,
        in_specs=[pl.BlockSpec(memory_space=vmem)] * 5,
        out_specs=[pl.BlockSpec(memory_space=vmem)] * 5,
        compiler_params=pltpu.CompilerParams(vmem_limit_bytes=60 * 1024 * 1024),
    )(*found)
    return mlp_out, input_grad, cheb_grad.reshape(ORDER, GROUP, 128), first_grad, second_grad.T


def solution(mesh):
    return jax.shard_map(
        body,
        mesh=mesh,
        in_specs=(
            P("chan", "region"),
            P(None, "region"),
            P(None, "region"),
            P(),
            P(None, "chan", None),
            P(None, "chan"),
            P("chan", None),
            P("chan", "region"),
        ),
        out_specs=(
            P("chan", "region"),
            P("chan", "region"),
            P(None, "chan", None),
            P(None, "chan"),
            P("chan", None),
        ),
        check_vma=False,
    )
```

```python
import math

import jax
import jax.numpy as jnp
from jax import lax
from jax.experimental import pallas as pl
from jax.experimental.pallas import tpu as pltpu
from jax.sharding import PartitionSpec as P

F32, BF16, I32 = jnp.float32, jnp.bfloat16, jnp.int32
MESH = pl.DeviceIdType.MESH
PIX, WW, ORDER, GROUP = 512, 128, 4, 32
NZ, NX, NXC, NCHAN, NREGION = 16, 4, 8, 4, 128
NPLANE = NXC * NCHAN
NDUO, TILE = 16, 16
OUT_PART, ROWS_DEV, OUTF = 16, 256, 64

W1, W2, W3, A1, A2, C0, DG, GS, B1, B2, G1, G2, F2, H1, H2, I2 = [*range(6), *range(9, 19)]
EXCHANGES = 19


def dot(left, right, left_dim=1, right_dim=0):
    return lax.dot_general(
        left, right, (((left_dim,), (right_dim,)), ((), ())), preferred_element_type=F32
    )


def iota(shape, dim):
    return lax.broadcasted_iota(I32, shape, dim)


def kernel(
    sky_in, nb_in, sl_in, cnt_in, cheb_in, w1_in, w2_in, cot_in,
    mo_out, ig_out, cg_out, fg_out, sg_out,
    sky, nb, sl, cnt, cheb, w1, w2, cot,
    amat, smat, mmat, emat, basis, hs, hr, wg1, wg2, s1, r1, s2, r2, wt, wgt, bs, bq,
    dg_s, dg, gs, gr, g1, rg1, g2, rg2, ft, fin, h1, rh1, h2, rh2, fs, fins,
    loads, hsend, hrecv, send, recv, h1send,
):
    region, chan = lax.axis_index("region"), lax.axis_index("chan")
    core, z, x = lax.rem(region, 2), lax.rem(lax.div(region, 2), NZ), lax.div(region, 2 * NZ)
    xc = x * 2 + core

    plane = xc * NCHAN + chan

    def z_peer(step):
        other = lax.rem(z + step, NZ)
        return other, ((x * NZ + other) * 2 + core, chan)

    def plane_peer(step):
        other = lax.rem(plane + step, NPLANE)
        there = lax.div(other, NCHAN)
        there = (lax.div(there, 2) * NZ + z) * 2 + lax.rem(there, 2)
        return other, (there, lax.rem(other, NCHAN))

    parity, z_pair = lax.rem(z, 2), lax.div(z, 2)
    duo = xc * 2 + parity
    holder = duo == x * 4

    def duo_device(other):
        there = lax.div(other, 4) * NZ + z_pair * 2 + lax.rem(other, 2)
        return there * 2 + lax.rem(lax.div(other, 2), 2), chan

    def duo_peer(step):
        other = lax.rem(duo + step, NDUO)
        return other, duo_device(other)

    def line_peer(step):
        other = lax.rem(z_pair + step, NZ // 2)
        return other, ((x * NZ + other * 2 + parity) * 2 + core, chan)

    def chan_peer(step):
        other = lax.rem(chan + step, NCHAN)
        return other, (region, other)

    lower = (lax.rem(region + NREGION - 1, NREGION), chan)
    upper = (lax.rem(region + 1, NREGION), chan)

    barrier = pltpu.get_barrier_semaphore()

    def greet(peer, count):
        def step(d, carry):
            pl.semaphore_signal(barrier, inc=1, device_id=peer(d)[1], device_id_type=MESH)
            return carry

        lax.fori_loop(1, count, step, 0)

    greet(z_peer, NZ)
    for device in (lower, upper):
        pl.semaphore_signal(barrier, inc=1, device_id=device, device_id_type=MESH)
    greet(duo_peer, NDUO)
    greet(plane_peer, NPLANE)

    pairs = (
        (nb_in, nb), (sl_in, sl), (sky_in, sky), (cnt_in, cnt),
        (cot_in, cot), (w1_in, w1), (w2_in, w2), (cheb_in, cheb),
    )
    load = {id(there): pltpu.make_async_copy(here, there, loads.at[i]) for i, (here, there) in enumerate(pairs)}
    for copy in load.values():
        copy.start()

    def loaded(*refs):
        for ref in refs:
            load[id(ref)].wait()

    def spread(key, peer, count, src_at, dst):
        def step(d, carry):
            slot, device = peer(d)
            pltpu.make_async_remote_copy(
                src_ref=src_at(slot), dst_ref=dst, send_sem=send.at[key],
                recv_sem=recv.at[key], device_id=device, device_id_type=MESH,
            ).start()
            return carry

        lax.fori_loop(1, count, step, 0)

    def await_bytes(ref, sem):
        pltpu.make_async_copy(ref, ref, sem).wait()

    loaded(nb, sl, sky)
    links = nb[...]
    inv = 1.0 / jnp.sqrt(
        jnp.maximum(jnp.sum((links != PIX + 2 * WW).astype(F32), axis=0, keepdims=True), 1.0)
    )
    slot_row = iota((PIX, WW), 0)
    for side in range(2):
        smat[:, side * WW : (side + 1) * WW] = (
            jnp.where(slot_row == sl[side : side + 1, :], 1.0, 0.0).astype(BF16)
        )

    def halo_copy(step, side):
        return pltpu.make_async_remote_copy(
            src_ref=hs.at[step, side], dst_ref=hr.at[step, 1 - side],
            send_sem=hsend.at[step, side], recv_sem=hrecv.at[step, 1 - side],
            device_id=(lower, upper)[side], device_id_type=MESH,
        )

    def rim(step, values):
        scaled = values * inv
        high = scaled.astype(BF16)
        edge = dot(high, smat[...]).astype(BF16)
        hs[step, 0] = edge[:, :WW]
        hs[step, 1] = edge[:, WW:]
        return scaled, high

    def halo_start(step):
        for side in range(2):
            halo_copy(step, side).start()

    def inner(pair):
        scaled, high = pair
        low = (scaled - high.astype(F32)).astype(BF16)
        both = dot(jnp.concatenate([high, low], axis=0), amat[:PIX])
        return both[:GROUP] + both[GROUP:]

    def finish(step, local):
        for side in range(2):
            halo_copy(step, 1 - side).wait_recv()
        local = local + dot(hr[step, 0], amat[PIX : PIX + WW])
        local = local + dot(hr[step, 1], amat[PIX + WW :])
        return -inv * local

    def keep(level, values):
        basis[level * GROUP : (level + 1) * GROUP] = values
        for s in range(NCHAN):
            bs[level, s] = values[:, s * WW : (s + 1) * WW]

    def share(level):
        spread(C0 + level, chan_peer, NCHAN, lambda slot: bs.at[level, slot], bq.at[chan, level])
        bq[chan, level] = bs[level, chan]

    v0 = sky[...].astype(F32)
    keep(0, sky[...])
    pair = rim(0, v0)

    loaded(cnt, cot)
    counts = cnt[...].astype(F32)
    own_start = jnp.sum(
        jnp.where(iota((64, NREGION), 1) < region, counts, 0.0), axis=1, keepdims=True
    )[:1].astype(I32)

    def places(order):
        lane = iota(order.shape, 1)
        count = jnp.sum(jnp.where(lane == order, counts, 0.0), axis=1, keepdims=True).astype(I32)
        start = jnp.sum(jnp.where(lane < order, counts, 0.0), axis=1, keepdims=True).astype(I32)
        off = (region - start) & (NREGION - 1)
        first = (start + off - region) >> 7
        return count, off, first

    def exchange1(k, message):
        s1[k] = message.reshape(NZ, NX, 128)

    def exchange1_start(k, key):
        spread(key, z_peer, NZ, lambda slot: s1.at[k, slot], r1.at[k, z])
        r1[k, z] = s1[k, z]

    def exchange2(k, key1, key2):
        await_bytes(r1.at[k, pl.ds(0, NZ - 1)], recv.at[key1])
        here = jnp.concatenate([r1[k, :, i, :] for i in range(NX)], axis=0).astype(BF16)
        moved = dot(here, emat[...]).astype(BF16)
        for i in range(NX):
            for b in range(2 * NCHAN):
                s2[k, i * 2 * NCHAN + b] = moved[i * NZ : (i + 1) * NZ, b * 128 : (b + 1) * 128]
        spread(key2, plane_peer, NPLANE, lambda slot: s2.at[k, slot], r2.at[k, plane])
        r2[k, plane] = s2[k, plane]

    def arrived2(k, key2):
        await_bytes(r2.at[k, pl.ds(0, NPLANE - 1)], recv.at[key2])
        parts = r2[k].astype(F32).reshape(NXC, NCHAN, NZ, 128)
        total = parts[:, 0]
        for s in range(1, NCHAN):
            total = total + parts[:, s]
        return total.reshape(NREGION, 128).T.astype(BF16)

    pair_row = iota((NZ * NX, NREGION), 0)
    zmajor = ((pair_row & 3) * NZ + (pair_row >> 2)) * 2
    count0, off0, first0 = places(zmajor)
    count1, off1, first1 = places(zmajor + 1)
    own_cot = cot[...].astype(F32)
    shifted = [own_cot] + [pltpu.roll(own_cot, ROWS_DEV - s, 1) for s in range(1, 4)]
    shifted = jnp.concatenate(shifted, axis=0).astype(BF16)
    empty = jnp.zeros_like(shifted)
    shifted = jnp.concatenate(
        [jnp.concatenate([shifted, empty], axis=1), jnp.concatenate([empty, shifted], axis=1)], axis=0
    )
    own_row = iota((NZ * NX, ROWS_DEV), 1)
    choice = jnp.concatenate([own_row == first0, own_row == first1], axis=1)
    message = dot(jnp.where(choice, 1.0, 0.0).astype(BF16), shifted, 1, 1)
    lane64 = iota((NZ * NX, NREGION), 1)
    room = jnp.where(lane64 < 64, count0 - off0, count1 - off1)
    message = jnp.where(((lane64 & 63) >> 4) * NREGION < room, message, 0.0)
    exchange1(0, message)
    gone = jnp.where(region == 0, 0, -1)
    gone_up = jnp.where(region == NREGION - 1, 0, -1)
    links = jnp.where((links >= PIX) & (links < PIX + WW) & (gone == 0), PIX + 2 * WW, links)
    links = jnp.where((links >= PIX + WW) & (gone_up == 0), PIX + 2 * WW, links)
    block_row = iota((32, PIX), 0)

    def build(b, carry):
        base = pl.multiple_of(b * 32, 32)
        near = links - base
        total = jnp.zeros((32, PIX), F32)
        for e in range(8):
            total = total + jnp.where(block_row == near[e : e + 1], 1.0, 0.0)
        amat[pl.ds(base, 32), :] = total.astype(BF16)
        return carry

    lax.fori_loop(0, (PIX + 2 * WW) // 32, build, 0)

    pl.semaphore_wait(barrier, 2 + (NPLANE - 1) + (NZ - 1) + (NDUO - 1))
    exchange1_start(0, A1)
    halo_start(0)
    loaded(w1, w2)
    spread(W1, chan_peer, NCHAN, lambda slot: w1, wg1.at[chan])
    spread(W2, chan_peer, NCHAN, lambda slot: w2, wg2.at[chan])

    loaded(cheb)
    weight = cheb[...]
    wt[...] = weight.astype(F32).T.astype(BF16)
    spread(W3, chan_peer, NCHAN, lambda slot: wt, wgt.at[chan])
    wg1[chan] = w1[...]
    wg2[chan] = w2[...]
    wgt[chan] = wt[...]

    share(0)
    local = inner(pair)
    from_row, to_lane = iota((128, 1024), 0), iota((128, 1024), 1)
    emat[...] = jnp.where(
        ((from_row >> 4) == (to_lane >> 7))
        & ((to_lane & 127) == chan * OUT_PART + (from_row & 15)),
        1.0, 0.0,
    ).astype(BF16)
    lane, row = iota((NREGION, NREGION), 1), iota((NREGION, NREGION), 0)
    xcmajor = (((row >> 5) * NZ + (row & 15)) * 2) + ((row >> 4) & 1)
    to_pixels = jnp.where(((xcmajor - own_start) & 127) == lane, 1.0, 0.0).astype(BF16)
    to_rows = jnp.concatenate(
        [((zmajor + i - own_start) & 127) == lane64 for i in range(2)], axis=1
    )
    to_rows = jnp.where(to_rows, 1.0, 0.0).astype(BF16)
    v1 = finish(0, local)
    pair = rim(1, v1)
    halo_start(1)
    keep(1, v1.astype(BF16))
    share(1)
    local = inner(pair)
    v2 = 2.0 * finish(1, local) - v0
    pair = rim(2, v2)
    halo_start(2)
    keep(2, v2.astype(BF16))
    share(2)
    local = inner(pair)
    exchange2(0, A1, A2)
    v3 = 2.0 * finish(2, local) - v1
    keep(3, v3.astype(BF16))
    share(3)

    await_bytes(wg2.at[pl.ds(0, NCHAN - 1)], recv.at[W2])
    await_bytes(wg1.at[pl.ds(0, NCHAN - 1)], recv.at[W1])
    await_bytes(wgt.at[pl.ds(0, NCHAN - 1)], recv.at[W3])
    for level in range(ORDER):
        await_bytes(bq.at[pl.ds(0, NCHAN - 1), level], recv.at[C0 + level])
    conv = jnp.zeros((128, WW), F32)
    for s in range(NCHAN):
        conv = conv + dot(wgt[s], bq[s].reshape(ORDER * GROUP, WW))
    features = conv.astype(BF16)
    features_t = conv.T.astype(BF16)
    hidden, slope = [], []
    out_t = jnp.zeros((WW, OUTF), F32)
    for h in range(NCHAN):
        pre = dot(features_t, wg1[h])
        gate = jax.nn.sigmoid(pre)
        hidden.append((pre * gate).astype(BF16))
        slope.append(gate * (1.0 + pre * (1.0 - gate)))

    columns = dot(arrived2(0, A2), to_pixels)[:OUTF]
    cot_px = columns.astype(BF16)
    cot_t = columns.T.astype(BF16)
    d_pre = []
    d_feat = jnp.zeros((WW, 128), F32)
    for h in range(NCHAN):
        d_pre.append((dot(cot_t, wg2[h]) * slope[h]).astype(BF16))
        d_feat = d_feat + dot(d_pre[h], wg1[h], 1, 1)
    dg_s[...] = d_feat.astype(BF16)
    spread(DG, chan_peer, NCHAN, lambda slot: dg_s, dg.at[chan])
    dg[chan] = dg_s[...]

    for h in range(NCHAN):
        gs[h, 0:128] = dot(features, d_pre[h]).astype(BF16)
        gs[h, 128:192] = dot(cot_px, hidden[h]).astype(BF16)
        out_t = out_t + dot(hidden[h], wg2[h], 1, 1)
    spread(GS, chan_peer, NCHAN, lambda slot: gs.at[slot], gr.at[chan])
    gr[chan] = gs[chan]
    outs = out_t.T.astype(BF16)
    empty = jnp.zeros_like(outs)
    outs = jnp.concatenate(
        [jnp.concatenate([outs, empty], axis=1), jnp.concatenate([empty, outs], axis=1)], axis=0
    )
    exchange1(1, dot(to_rows, outs, 1, 1))
    exchange1_start(1, B1)

    await_bytes(dg.at[pl.ds(0, NCHAN - 1)], recv.at[DG])
    d_conv_t = dg[...].reshape(PIX, 128)
    cheb_part = dot(basis[...], d_conv_t)
    for i in range(NXC):
        g1[2 * i] = cheb_part[TILE * i : TILE * (i + 1)].astype(BF16)

    def to_half(half):
        def step(d, carry):
            other = 2 * d + half

            @pl.when(other != duo)
            def _():
                pltpu.make_async_remote_copy(
                    src_ref=g1.at[other], dst_ref=rg1.at[duo], send_sem=send.at[G1],
                    recv_sem=recv.at[G1], device_id=duo_device(other), device_id_type=MESH,
                ).start()

            return carry

        lax.fori_loop(0, NDUO // 2, step, 0)

    to_half(0)
    adj3 = dot(weight[3 * GROUP :], d_conv_t, 1, 1)
    pair = rim(3, adj3)
    halo_start(3)
    await_bytes(gr.at[pl.ds(0, NCHAN - 1)], recv.at[GS])
    grads = gr[0].astype(F32)
    for s in range(1, NCHAN):
        grads = grads + gr[s].astype(F32)
    for i in range(NXC):
        g1[2 * i + 1] = grads[TILE * i : TILE * (i + 1)].astype(BF16)
    to_half(1)
    for i in range(NX):
        h1[i] = grads[128 + TILE * i : 128 + TILE * (i + 1)].astype(BF16)

    def to_holder(i):
        return pltpu.make_async_remote_copy(
            src_ref=h1.at[i], dst_ref=rh1.at[duo], send_sem=h1send.at[i], recv_sem=recv.at[H1],
            device_id=duo_device(4 * i), device_id_type=MESH,
        )

    for i in range(NX):
        @pl.when(duo != 4 * i)
        def _(i=i):
            to_holder(i).start()

        @pl.when(duo == 4 * i)
        def _(i=i):
            rh1[duo] = h1[i]

    rg1[duo] = g1[duo]
    local = inner(pair)
    d_low = dot(weight[: 3 * GROUP], d_conv_t, 1, 1)
    adj2 = d_low[2 * GROUP :] + 2.0 * finish(3, local)
    adj1 = d_low[GROUP : 2 * GROUP] - adj3
    pair = rim(4, adj2)
    halo_start(4)

    def sum_of(ref, count):
        total = ref[0].astype(F32)
        for s in range(1, count):
            total = total + ref[s].astype(F32)
        return total.astype(BF16)

    await_bytes(rg1.at[pl.ds(0, NDUO - 1)], recv.at[G1])
    g2[...] = sum_of(rg1, NDUO)
    spread(G2, line_peer, NZ // 2, lambda slot: g2, rg2.at[z_pair])
    rg2[z_pair] = g2[...]

    @pl.when(holder)
    def _():
        await_bytes(rh1.at[pl.ds(0, NDUO - 1)], recv.at[H1])
        h2[...] = sum_of(rh1, NDUO)
        spread(H2, line_peer, NZ // 2, lambda slot: h2, rh2.at[z_pair])
        rh2[z_pair] = h2[...]

    exchange2(1, B1, B2)
    local = inner(pair)
    count2, off2, first2 = places(xcmajor)
    out_row = iota((NREGION, ROWS_DEV), 1)
    for s in range(4):
        fine = (out_row == first2 + s) & (off2 + s * NREGION < count2)
        mmat[s] = jnp.where(fine, 1.0, 0.0).astype(BF16)
    adj1 = adj1 + 2.0 * finish(4, local)
    adj0 = d_low[:GROUP] - adj2
    pair = rim(5, adj1)
    halo_start(5)

    local = inner(pair)
    ig_out[...] = adj0 + finish(5, local)

    rows_t = arrived2(1, B2)
    result = jnp.zeros((OUT_PART, ROWS_DEV), F32)
    for s in range(4):
        result = result + dot(rows_t[s * OUT_PART : (s + 1) * OUT_PART], mmat[s])
    mo_out[...] = result.astype(BF16)

    await_bytes(rg2.at[pl.ds(0, NZ // 2 - 1)], recv.at[G2])
    ft[...] = sum_of(rg2, NZ // 2)
    spread(F2, duo_peer, NDUO, lambda slot: ft, fin.at[duo])
    fin[duo] = ft[...]

    @pl.when(holder)
    def _():
        await_bytes(rh2.at[pl.ds(0, NZ // 2 - 1)], recv.at[H2])
        fs[...] = sum_of(rh2, NZ // 2)
        spread(I2, duo_peer, NDUO, lambda slot: fs, fins.at[x])
        fins[x] = fs[...]
        await_bytes(fins.at[pl.ds(0, NX - 1)], recv.at[I2])

    @pl.when(jnp.logical_not(holder))
    def _():
        await_bytes(fins, recv.at[I2])

    scale = 1.0 / math.sqrt(NREGION * ROWS_DEV)
    await_bytes(fin.at[pl.ds(0, NDUO - 1)], recv.at[F2])
    for i in range(NXC):
        cg_out[TILE * i : TILE * (i + 1)] = fin[2 * i].astype(F32) * scale
        fg_out[TILE * i : TILE * (i + 1)] = fin[2 * i + 1].astype(F32) * scale
    sg_out[...] = fins[...].astype(F32).reshape(OUTF, 128) * scale

    for step in range(6):
        for side in range(2):
            halo_copy(step, side).wait_send()
    for key, ref in ((W1, wg1), (W2, wg2), (W3, wgt), (DG, dg), (GS, gr)):
        await_bytes(ref.at[pl.ds(0, NCHAN - 1)], send.at[key])
    for level in range(ORDER):
        await_bytes(bq.at[pl.ds(0, NCHAN - 1), level], send.at[C0 + level])
    for k, key1, key2 in ((0, A1, A2), (1, B1, B2)):
        await_bytes(r1.at[k, pl.ds(0, NZ - 1)], send.at[key1])
        await_bytes(r2.at[k, pl.ds(0, NPLANE - 1)], send.at[key2])
    await_bytes(rg1.at[pl.ds(0, NDUO - 1)], send.at[G1])
    await_bytes(rg2.at[pl.ds(0, NZ // 2 - 1)], send.at[G2])
    await_bytes(fin.at[pl.ds(0, NDUO - 1)], send.at[F2])
    for i in range(NX):
        @pl.when(duo != 4 * i)
        def _(i=i):
            to_holder(i).wait_send()

    @pl.when(holder)
    def _():
        await_bytes(rh2.at[pl.ds(0, NZ // 2 - 1)], send.at[H2])
        await_bytes(rh1.at[pl.ds(0, NDUO - 1)], send.at[I2])


def writer(*refs):
    count = len(refs) // 2
    for i in range(count):
        refs[count + i][...] = refs[i][...]


def body(
    sky_maps, neighbours, send_lists, counts, cheb_weight, first_weight, second_weight, cotangent
):
    dma = pltpu.SemaphoreType.DMA
    vmem = pltpu.VMEM
    shape = jax.ShapeDtypeStruct
    args = (
        sky_maps,
        neighbours,
        send_lists,
        counts.reshape(1, NREGION),
        cheb_weight.reshape(ORDER * GROUP, 128),
        first_weight,
        second_weight.T,
        cotangent,
    )
    scratch = [vmem(arg.shape, arg.dtype) for arg in args] + [
        vmem((PIX + 2 * WW, PIX), BF16),
        vmem((PIX, 2 * WW), BF16),
        vmem((4, NREGION, ROWS_DEV), BF16),
        vmem((128, 1024), BF16),
        vmem((ORDER * GROUP, PIX), BF16),
        vmem((6, 2, GROUP, WW), BF16),
        vmem((6, 2, GROUP, WW), BF16),
        vmem((NCHAN, 128, 128), BF16),
        vmem((NCHAN, OUTF, 128), BF16),
        vmem((2, NZ, NX, 128), F32),
        vmem((2, NZ, NX, 128), F32),
        vmem((2, NPLANE, NZ, 128), BF16),
        vmem((2, NPLANE, NZ, 128), BF16),
        vmem((128, ORDER * GROUP), BF16),
        vmem((NCHAN, 128, ORDER * GROUP), BF16),
        vmem((ORDER, NCHAN, GROUP, WW), BF16),
        vmem((NCHAN, ORDER, GROUP, WW), BF16),
        vmem((WW, 128), BF16),
        vmem((NCHAN, WW, 128), BF16),
        vmem((NCHAN, 192, 128), BF16),
        vmem((NCHAN, 192, 128), BF16),
        vmem((NDUO, TILE, 128), BF16),
        vmem((NDUO, TILE, 128), BF16),
        vmem((TILE, 128), BF16),
        vmem((NZ // 2, TILE, 128), BF16),
        vmem((TILE, 128), BF16),
        vmem((NDUO, TILE, 128), BF16),
        vmem((NX, TILE, 128), BF16),
        vmem((NDUO, TILE, 128), BF16),
        vmem((TILE, 128), BF16),
        vmem((NZ // 2, TILE, 128), BF16),
        vmem((TILE, 128), BF16),
        vmem((NX, TILE, 128), BF16),
        dma((8,)),
        dma((6, 2)),
        dma((6, 2)),
        dma((EXCHANGES,)),
        dma((EXCHANGES,)),
        dma((NX,)),
    ]
    results = (
        shape((OUT_PART, ROWS_DEV), BF16),
        shape((GROUP, PIX), F32),
        shape((ORDER * GROUP, 128), F32),
        shape((128, 128), F32),
        shape((OUTF, 128), F32),
    )
    found = pl.pallas_call(
        kernel,
        out_shape=results,
        in_specs=[pl.BlockSpec(memory_space=pl.ANY)] * 8,
        out_specs=[pl.BlockSpec(memory_space=vmem)] * 5,
        scratch_shapes=scratch,
        compiler_params=pltpu.CompilerParams(
            collective_id=0, has_side_effects=True, vmem_limit_bytes=60 * 1024 * 1024
        ),
        cost_estimate=pl.CostEstimate(
            flops=600_000_000, bytes_accessed=1_000_000, transcendentals=65_536
        ),
    )(*args)
    mlp_out, input_grad, cheb_grad, first_grad, second_grad = pl.pallas_call(
        writer,
        out_shape=results,
        in_specs=[pl.BlockSpec(memory_space=vmem)] * 5,
        out_specs=[pl.BlockSpec(memory_space=vmem)] * 5,
        compiler_params=pltpu.CompilerParams(vmem_limit_bytes=60 * 1024 * 1024),
    )(*found)
    return mlp_out, input_grad, cheb_grad.reshape(ORDER, GROUP, 128), first_grad, second_grad.T


def solution(mesh):
    return jax.shard_map(
        body,
        mesh=mesh,
        in_specs=(
            P("chan", "region"),
            P(None, "region"),
            P(None, "region"),
            P(),
            P(None, "chan", None),
            P(None, "chan"),
            P("chan", None),
            P("chan", "region"),
        ),
        out_specs=(
            P("chan", "region"),
            P("chan", "region"),
            P(None, "chan", None),
            P(None, "chan"),
            P("chan", None),
        ),
        check_vma=False,
    )
```

```python
import math

import jax
import jax.numpy as jnp
from jax import lax
from jax.experimental import pallas as pl
from jax.experimental.pallas import tpu as pltpu
from jax.sharding import PartitionSpec as P

F32, BF16, I32 = jnp.float32, jnp.bfloat16, jnp.int32
MESH = pl.DeviceIdType.MESH
PIX, WW, ORDER, GROUP = 512, 128, 4, 32
NZ, NX, NXC, NCHAN, NREGION = 16, 4, 8, 4, 128
NPLANE = NXC * NCHAN
NDUO, NQUAD, TILE = 16, 64, 16
OUT_PART, ROWS_DEV, OUTF = 16, 256, 64

W1, W2, W3, A1, A2, C0, DG, GS, B1, B2, G1, G2, F2, H1, H2, I2 = [*range(6), *range(9, 19)]
EXCHANGES = 19


def dot(left, right, left_dim=1, right_dim=0):
    return lax.dot_general(
        left, right, (((left_dim,), (right_dim,)), ((), ())), preferred_element_type=F32
    )


def iota(shape, dim):
    return lax.broadcasted_iota(I32, shape, dim)


def kernel(
    sky_in, nb_in, sl_in, cnt_in, cheb_in, w1_in, w2_in, cot_in,
    mo_out, ig_out, cg_out, fg_out, sg_out,
    sky, nb, sl, cnt, cheb, w1, w2, cot,
    amat, smat, mmat, emat, basis, hs, hr, wg1, wg2, s1, r1, s2, r2, wt, wgt, bs, bq,
    dg_s, dg, gs, gr, g1, rg1, g2, rg2, ft, fin, h1, rh1, h2, rh2, fs, fins,
    loads, hsend, hrecv, send, recv,
):
    region, chan = lax.axis_index("region"), lax.axis_index("chan")
    core, z, x = lax.rem(region, 2), lax.rem(lax.div(region, 2), NZ), lax.div(region, 2 * NZ)
    xc = x * 2 + core

    plane = xc * NCHAN + chan

    def z_peer(step):
        other = lax.rem(z + step, NZ)
        return other, ((x * NZ + other) * 2 + core, chan)

    def plane_peer(step):
        other = lax.rem(plane + step, NPLANE)
        there = lax.div(other, NCHAN)
        there = (lax.div(there, 2) * NZ + z) * 2 + lax.rem(there, 2)
        return other, (there, lax.rem(other, NCHAN))

    parity, z_pair = lax.rem(z, 2), lax.div(z, 2)
    duo = xc * 2 + parity
    holder = duo == x * 4

    def duo_device(other):
        there = lax.div(other, 4) * NZ + z_pair * 2 + lax.rem(other, 2)
        return there * 2 + lax.rem(lax.div(other, 2), 2), chan

    def duo_peer(step):
        other = lax.rem(duo + step, NDUO)
        return other, duo_device(other)

    quad = duo * NCHAN + chan

    def quad_device(there, other_chan):
        return duo_device(there)[0], other_chan

    def quad_peer(step):
        other = lax.rem(quad + step, NQUAD)
        return other, quad_device(lax.div(other, NCHAN), lax.rem(other, NCHAN))

    def line_peer(step):
        other = lax.rem(z_pair + step, NZ // 2)
        return other, ((x * NZ + other * 2 + parity) * 2 + core, chan)

    def chan_peer(step):
        other = lax.rem(chan + step, NCHAN)
        return other, (region, other)

    lower = (lax.rem(region + NREGION - 1, NREGION), chan)
    upper = (lax.rem(region + 1, NREGION), chan)

    barrier = pltpu.get_barrier_semaphore()

    def greet(peer, count):
        def step(d, carry):
            pl.semaphore_signal(barrier, inc=1, device_id=peer(d)[1], device_id_type=MESH)
            return carry

        lax.fori_loop(1, count, step, 0)

    greet(z_peer, NZ)
    for device in (lower, upper):
        pl.semaphore_signal(barrier, inc=1, device_id=device, device_id_type=MESH)
    greet(quad_peer, NQUAD)

    pairs = (
        (nb_in, nb), (sl_in, sl), (sky_in, sky), (cnt_in, cnt),
        (cot_in, cot), (w1_in, w1), (w2_in, w2), (cheb_in, cheb),
    )
    load = {id(there): pltpu.make_async_copy(here, there, loads.at[i]) for i, (here, there) in enumerate(pairs)}
    for copy in load.values():
        copy.start()

    def loaded(*refs):
        for ref in refs:
            load[id(ref)].wait()

    def spread(key, peer, count, src_at, dst):
        def step(d, carry):
            slot, device = peer(d)
            pltpu.make_async_remote_copy(
                src_ref=src_at(slot), dst_ref=dst, send_sem=send.at[key],
                recv_sem=recv.at[key], device_id=device, device_id_type=MESH,
            ).start()
            return carry

        lax.fori_loop(1, count, step, 0)

    def await_bytes(ref, sem):
        pltpu.make_async_copy(ref, ref, sem).wait()

    loaded(nb, sl, sky)
    links = nb[...]
    inv = 1.0 / jnp.sqrt(
        jnp.maximum(jnp.sum((links != PIX + 2 * WW).astype(F32), axis=0, keepdims=True), 1.0)
    )
    slot_row = iota((PIX, WW), 0)
    for side in range(2):
        smat[:, side * WW : (side + 1) * WW] = (
            jnp.where(slot_row == sl[side : side + 1, :], 1.0, 0.0).astype(BF16)
        )

    def halo_copy(step, side):
        return pltpu.make_async_remote_copy(
            src_ref=hs.at[step, side], dst_ref=hr.at[step, 1 - side],
            send_sem=hsend.at[step, side], recv_sem=hrecv.at[step, 1 - side],
            device_id=(lower, upper)[side], device_id_type=MESH,
        )

    def rim(step, values):
        scaled = values * inv
        high = scaled.astype(BF16)
        edge = dot(high, smat[...]).astype(BF16)
        hs[step, 0] = edge[:, :WW]
        hs[step, 1] = edge[:, WW:]
        return scaled, high

    def halo_start(step):
        for side in range(2):
            halo_copy(step, side).start()

    def inner(pair):
        scaled, high = pair
        low = (scaled - high.astype(F32)).astype(BF16)
        both = dot(jnp.concatenate([high, low], axis=0), amat[:PIX])
        return both[:GROUP] + both[GROUP:]

    def finish(step, local):
        for side in range(2):
            halo_copy(step, 1 - side).wait_recv()
        local = local + dot(hr[step, 0], amat[PIX : PIX + WW])
        local = local + dot(hr[step, 1], amat[PIX + WW :])
        return -inv * local

    def keep(level, values):
        basis[level * GROUP : (level + 1) * GROUP] = values
        for s in range(NCHAN):
            bs[level, s] = values[:, s * WW : (s + 1) * WW]

    def share(level):
        spread(C0 + level, chan_peer, NCHAN, lambda slot: bs.at[level, slot], bq.at[chan, level])
        bq[chan, level] = bs[level, chan]

    v0 = sky[...].astype(F32)
    keep(0, sky[...])
    pair = rim(0, v0)

    loaded(cnt, cot)
    counts = cnt[...].astype(F32)
    own_start = jnp.sum(
        jnp.where(iota((64, NREGION), 1) < region, counts, 0.0), axis=1, keepdims=True
    )[:1].astype(I32)

    def places(order):
        lane = iota(order.shape, 1)
        count = jnp.sum(jnp.where(lane == order, counts, 0.0), axis=1, keepdims=True).astype(I32)
        start = jnp.sum(jnp.where(lane < order, counts, 0.0), axis=1, keepdims=True).astype(I32)
        off = (region - start) & (NREGION - 1)
        first = (start + off - region) >> 7
        return count, off, first

    def exchange1(k, message):
        s1[k] = message.reshape(NZ, NX, 128)

    def exchange1_start(k, key):
        spread(key, z_peer, NZ, lambda slot: s1.at[k, slot], r1.at[k, z])
        r1[k, z] = s1[k, z]

    def exchange2(k, key1, key2):
        await_bytes(r1.at[k, pl.ds(0, NZ - 1)], recv.at[key1])
        here = jnp.concatenate([r1[k, :, i, :] for i in range(NX)], axis=0).astype(BF16)
        moved = dot(here, emat[...]).astype(BF16)
        for i in range(NX):
            for b in range(2 * NCHAN):
                s2[k, i * 2 * NCHAN + b] = moved[i * NZ : (i + 1) * NZ, b * 128 : (b + 1) * 128]
        spread(key2, plane_peer, NPLANE, lambda slot: s2.at[k, slot], r2.at[k, plane])
        r2[k, plane] = s2[k, plane]

    def arrived2(k, key2):
        await_bytes(r2.at[k, pl.ds(0, NPLANE - 1)], recv.at[key2])
        parts = r2[k].astype(F32).reshape(NXC, NCHAN, NZ, 128)
        total = parts[:, 0]
        for s in range(1, NCHAN):
            total = total + parts[:, s]
        return total.reshape(NREGION, 128).T.astype(BF16)

    pair_row = iota((NZ * NX, NREGION), 0)
    zmajor = ((pair_row & 3) * NZ + (pair_row >> 2)) * 2
    count0, off0, first0 = places(zmajor)
    count1, off1, first1 = places(zmajor + 1)
    own_cot = cot[...].astype(F32)
    shifted = [own_cot] + [pltpu.roll(own_cot, ROWS_DEV - s, 1) for s in range(1, 4)]
    shifted = jnp.concatenate(shifted, axis=0).astype(BF16)
    empty = jnp.zeros_like(shifted)
    shifted = jnp.concatenate(
        [jnp.concatenate([shifted, empty], axis=1), jnp.concatenate([empty, shifted], axis=1)], axis=0
    )
    own_row = iota((NZ * NX, ROWS_DEV), 1)
    choice = jnp.concatenate([own_row == first0, own_row == first1], axis=1)
    message = dot(jnp.where(choice, 1.0, 0.0).astype(BF16), shifted, 1, 1)
    lane64 = iota((NZ * NX, NREGION), 1)
    room = jnp.where(lane64 < 64, count0 - off0, count1 - off1)
    message = jnp.where(((lane64 & 63) >> 4) * NREGION < room, message, 0.0)
    exchange1(0, message)
    gone = jnp.where(region == 0, 0, -1)
    gone_up = jnp.where(region == NREGION - 1, 0, -1)
    links = jnp.where((links >= PIX) & (links < PIX + WW) & (gone == 0), PIX + 2 * WW, links)
    links = jnp.where((links >= PIX + WW) & (gone_up == 0), PIX + 2 * WW, links)
    block_row = iota((32, PIX), 0)

    def build(b, carry):
        base = pl.multiple_of(b * 32, 32)
        near = links - base
        total = jnp.zeros((32, PIX), F32)
        for e in range(8):
            total = total + jnp.where(block_row == near[e : e + 1], 1.0, 0.0)
        amat[pl.ds(base, 32), :] = total.astype(BF16)
        return carry

    lax.fori_loop(0, (PIX + 2 * WW) // 32, build, 0)

    pl.semaphore_wait(barrier, 2 + (NQUAD - 1) + (NZ - 1))
    exchange1_start(0, A1)
    halo_start(0)
    loaded(w1, w2)
    spread(W1, chan_peer, NCHAN, lambda slot: w1, wg1.at[chan])
    spread(W2, chan_peer, NCHAN, lambda slot: w2, wg2.at[chan])

    loaded(cheb)
    weight = cheb[...]
    wt[...] = weight.astype(F32).T.astype(BF16)
    spread(W3, chan_peer, NCHAN, lambda slot: wt, wgt.at[chan])
    wg1[chan] = w1[...]
    wg2[chan] = w2[...]
    wgt[chan] = wt[...]

    share(0)
    local = inner(pair)
    from_row, to_lane = iota((128, 1024), 0), iota((128, 1024), 1)
    emat[...] = jnp.where(
        ((from_row >> 4) == (to_lane >> 7))
        & ((to_lane & 127) == chan * OUT_PART + (from_row & 15)),
        1.0, 0.0,
    ).astype(BF16)
    lane, row = iota((NREGION, NREGION), 1), iota((NREGION, NREGION), 0)
    xcmajor = (((row >> 5) * NZ + (row & 15)) * 2) + ((row >> 4) & 1)
    to_pixels = jnp.where(((xcmajor - own_start) & 127) == lane, 1.0, 0.0).astype(BF16)
    to_rows = jnp.concatenate(
        [((zmajor + i - own_start) & 127) == lane64 for i in range(2)], axis=1
    )
    to_rows = jnp.where(to_rows, 1.0, 0.0).astype(BF16)
    v1 = finish(0, local)
    pair = rim(1, v1)
    halo_start(1)
    keep(1, v1.astype(BF16))
    share(1)
    local = inner(pair)
    v2 = 2.0 * finish(1, local) - v0
    pair = rim(2, v2)
    halo_start(2)
    keep(2, v2.astype(BF16))
    share(2)
    local = inner(pair)
    exchange2(0, A1, A2)
    v3 = 2.0 * finish(2, local) - v1
    keep(3, v3.astype(BF16))
    share(3)

    await_bytes(wg2.at[pl.ds(0, NCHAN - 1)], recv.at[W2])
    await_bytes(wg1.at[pl.ds(0, NCHAN - 1)], recv.at[W1])
    await_bytes(wgt.at[pl.ds(0, NCHAN - 1)], recv.at[W3])
    for level in range(ORDER):
        await_bytes(bq.at[pl.ds(0, NCHAN - 1), level], recv.at[C0 + level])
    conv = jnp.zeros((128, WW), F32)
    for s in range(NCHAN):
        conv = conv + dot(wgt[s], bq[s].reshape(ORDER * GROUP, WW))
    features = conv.astype(BF16)
    features_t = conv.T.astype(BF16)
    hidden, slope = [], []
    out_t = jnp.zeros((WW, OUTF), F32)
    for h in range(NCHAN):
        pre = dot(features_t, wg1[h])
        gate = jax.nn.sigmoid(pre)
        hidden.append((pre * gate).astype(BF16))
        slope.append(gate * (1.0 + pre * (1.0 - gate)))

    columns = dot(arrived2(0, A2), to_pixels)[:OUTF]
    cot_px = columns.astype(BF16)
    cot_t = columns.T.astype(BF16)
    d_pre = []
    d_feat = jnp.zeros((WW, 128), F32)
    for h in range(NCHAN):
        d_pre.append((dot(cot_t, wg2[h]) * slope[h]).astype(BF16))
        d_feat = d_feat + dot(d_pre[h], wg1[h], 1, 1)
    dg_s[...] = d_feat.astype(BF16)
    spread(DG, chan_peer, NCHAN, lambda slot: dg_s, dg.at[chan])
    dg[chan] = dg_s[...]

    for h in range(NCHAN):
        first = dot(features, d_pre[h]).astype(BF16)
        second = dot(cot_px, hidden[h]).astype(BF16)
        out_t = out_t + dot(hidden[h], wg2[h], 1, 1)
        for i in range(NXC):
            gs[i * NCHAN + h] = first[TILE * i : TILE * (i + 1)]
        for i in range(NX):
            h1[i * NCHAN + h] = second[TILE * i : TILE * (i + 1)]

    def scatter(key, count, mine, duo_of, src, dst):
        def step(d, carry):
            slot = lax.rem(mine + d, count)
            there, other_chan = duo_of(lax.div(slot, NCHAN)), lax.rem(slot, NCHAN)

            @pl.when(there * NCHAN + other_chan != quad)
            def _():
                pltpu.make_async_remote_copy(
                    src_ref=src.at[slot], dst_ref=dst.at[quad], send_sem=send.at[key],
                    recv_sem=recv.at[key], device_id=quad_device(there, other_chan),
                    device_id_type=MESH,
                ).start()

            return carry

        lax.fori_loop(0, count, step, 0)

    scatter(GS, NPLANE, plane, lambda i: 2 * i + 1, gs, gr)
    scatter(H1, NX * NCHAN, x * NCHAN + chan, lambda i: 4 * i, h1, rh1)

    @pl.when(parity == 1)
    def _():
        gr[quad] = gs[plane]

    @pl.when(holder)
    def _():
        rh1[quad] = h1[x * NCHAN + chan]

    outs = out_t.T.astype(BF16)
    empty = jnp.zeros_like(outs)
    outs = jnp.concatenate(
        [jnp.concatenate([outs, empty], axis=1), jnp.concatenate([empty, outs], axis=1)], axis=0
    )
    exchange1(1, dot(to_rows, outs, 1, 1))
    exchange1_start(1, B1)

    await_bytes(dg.at[pl.ds(0, NCHAN - 1)], recv.at[DG])
    d_conv_t = dg[...].reshape(PIX, 128)
    cheb_part = dot(basis[...], d_conv_t)
    for i in range(NXC):
        g1[i] = cheb_part[TILE * i : TILE * (i + 1)].astype(BF16)

    def cheb_step(d, carry):
        slot = lax.rem(xc + d, NXC)

        @pl.when(2 * slot != duo)
        def _():
            pltpu.make_async_remote_copy(
                src_ref=g1.at[slot], dst_ref=rg1.at[duo], send_sem=send.at[G1],
                recv_sem=recv.at[G1], device_id=duo_device(2 * slot), device_id_type=MESH,
            ).start()

        return carry

    lax.fori_loop(0, NXC, cheb_step, 0)

    @pl.when(parity == 0)
    def _():
        rg1[duo] = g1[xc]

    adj3 = dot(weight[3 * GROUP :], d_conv_t, 1, 1)
    pair = rim(3, adj3)
    halo_start(3)
    local = inner(pair)
    d_low = dot(weight[: 3 * GROUP], d_conv_t, 1, 1)
    adj2 = d_low[2 * GROUP :] + 2.0 * finish(3, local)
    adj1 = d_low[GROUP : 2 * GROUP] - adj3
    pair = rim(4, adj2)
    halo_start(4)

    def sum_of(ref, count):
        total = ref[0].astype(F32)
        for s in range(1, count):
            total = total + ref[s].astype(F32)
        return total.astype(BF16)

    @pl.when(parity == 0)
    def _():
        await_bytes(rg1.at[pl.ds(0, NDUO - 1)], recv.at[G1])
        g2[...] = sum_of(rg1, NDUO)

    @pl.when(parity == 1)
    def _():
        await_bytes(gr.at[pl.ds(0, NQUAD - 1)], recv.at[GS])
        g2[...] = sum_of(gr, NQUAD)

    spread(G2, line_peer, NZ // 2, lambda slot: g2, rg2.at[z_pair])
    rg2[z_pair] = g2[...]

    @pl.when(holder)
    def _():
        await_bytes(rh1.at[pl.ds(0, NQUAD - 1)], recv.at[H1])
        h2[...] = sum_of(rh1, NQUAD)
        spread(H2, line_peer, NZ // 2, lambda slot: h2, rh2.at[z_pair])
        rh2[z_pair] = h2[...]

    exchange2(1, B1, B2)
    local = inner(pair)
    count2, off2, first2 = places(xcmajor)
    out_row = iota((NREGION, ROWS_DEV), 1)
    for s in range(4):
        fine = (out_row == first2 + s) & (off2 + s * NREGION < count2)
        mmat[s] = jnp.where(fine, 1.0, 0.0).astype(BF16)
    adj1 = adj1 + 2.0 * finish(4, local)
    adj0 = d_low[:GROUP] - adj2
    pair = rim(5, adj1)
    halo_start(5)

    local = inner(pair)
    ig_out[...] = adj0 + finish(5, local)

    rows_t = arrived2(1, B2)
    result = jnp.zeros((OUT_PART, ROWS_DEV), F32)
    for s in range(4):
        result = result + dot(rows_t[s * OUT_PART : (s + 1) * OUT_PART], mmat[s])
    mo_out[...] = result.astype(BF16)

    await_bytes(rg2.at[pl.ds(0, NZ // 2 - 1)], recv.at[G2])
    ft[...] = sum_of(rg2, NZ // 2)
    spread(F2, duo_peer, NDUO, lambda slot: ft, fin.at[duo])
    fin[duo] = ft[...]

    @pl.when(holder)
    def _():
        await_bytes(rh2.at[pl.ds(0, NZ // 2 - 1)], recv.at[H2])
        fs[...] = sum_of(rh2, NZ // 2)
        spread(I2, duo_peer, NDUO, lambda slot: fs, fins.at[x])
        fins[x] = fs[...]
        await_bytes(fins.at[pl.ds(0, NX - 1)], recv.at[I2])

    @pl.when(jnp.logical_not(holder))
    def _():
        await_bytes(fins, recv.at[I2])

    scale = 1.0 / math.sqrt(NREGION * ROWS_DEV)
    await_bytes(fin.at[pl.ds(0, NDUO - 1)], recv.at[F2])
    for i in range(NXC):
        cg_out[TILE * i : TILE * (i + 1)] = fin[2 * i].astype(F32) * scale
        fg_out[TILE * i : TILE * (i + 1)] = fin[2 * i + 1].astype(F32) * scale
    sg_out[...] = fins[...].astype(F32).reshape(OUTF, 128) * scale

    for step in range(6):
        for side in range(2):
            halo_copy(step, side).wait_send()
    for key, ref in ((W1, wg1), (W2, wg2), (W3, wgt), (DG, dg)):
        await_bytes(ref.at[pl.ds(0, NCHAN - 1)], send.at[key])
    for level in range(ORDER):
        await_bytes(bq.at[pl.ds(0, NCHAN - 1), level], send.at[C0 + level])
    for k, key1, key2 in ((0, A1, A2), (1, B1, B2)):
        await_bytes(r1.at[k, pl.ds(0, NZ - 1)], send.at[key1])
        await_bytes(r2.at[k, pl.ds(0, NPLANE - 1)], send.at[key2])
    for own_parity in range(2):
        @pl.when(parity == own_parity)
        def _(own_parity=own_parity):
            await_bytes(rg1.at[pl.ds(0, NXC - 1 + own_parity)], send.at[G1])
            await_bytes(gr.at[pl.ds(0, NPLANE - own_parity)], send.at[GS])

    await_bytes(rg2.at[pl.ds(0, NZ // 2 - 1)], send.at[G2])
    await_bytes(fin.at[pl.ds(0, NDUO - 1)], send.at[F2])
    @pl.when(jnp.logical_not(holder))
    def _():
        await_bytes(rh1.at[pl.ds(0, NX * NCHAN)], send.at[H1])

    @pl.when(holder)
    def _():
        await_bytes(rh1.at[pl.ds(0, NX * NCHAN - 1)], send.at[H1])
        await_bytes(rh2.at[pl.ds(0, NZ // 2 - 1)], send.at[H2])
        await_bytes(rh1.at[pl.ds(0, NDUO - 1)], send.at[I2])


def writer(*refs):
    count = len(refs) // 2
    for i in range(count):
        refs[count + i][...] = refs[i][...]


def body(
    sky_maps, neighbours, send_lists, counts, cheb_weight, first_weight, second_weight, cotangent
):
    dma = pltpu.SemaphoreType.DMA
    vmem = pltpu.VMEM
    shape = jax.ShapeDtypeStruct
    args = (
        sky_maps,
        neighbours,
        send_lists,
        counts.reshape(1, NREGION),
        cheb_weight.reshape(ORDER * GROUP, 128),
        first_weight,
        second_weight.T,
        cotangent,
    )
    scratch = [vmem(arg.shape, arg.dtype) for arg in args] + [
        vmem((PIX + 2 * WW, PIX), BF16),
        vmem((PIX, 2 * WW), BF16),
        vmem((4, NREGION, ROWS_DEV), BF16),
        vmem((128, 1024), BF16),
        vmem((ORDER * GROUP, PIX), BF16),
        vmem((6, 2, GROUP, WW), BF16),
        vmem((6, 2, GROUP, WW), BF16),
        vmem((NCHAN, 128, 128), BF16),
        vmem((NCHAN, OUTF, 128), BF16),
        vmem((2, NZ, NX, 128), F32),
        vmem((2, NZ, NX, 128), F32),
        vmem((2, NPLANE, NZ, 128), BF16),
        vmem((2, NPLANE, NZ, 128), BF16),
        vmem((128, ORDER * GROUP), BF16),
        vmem((NCHAN, 128, ORDER * GROUP), BF16),
        vmem((ORDER, NCHAN, GROUP, WW), BF16),
        vmem((NCHAN, ORDER, GROUP, WW), BF16),
        vmem((WW, 128), BF16),
        vmem((NCHAN, WW, 128), BF16),
        vmem((NPLANE, TILE, 128), BF16),
        vmem((NQUAD, TILE, 128), BF16),
        vmem((NXC, TILE, 128), BF16),
        vmem((NDUO, TILE, 128), BF16),
        vmem((TILE, 128), BF16),
        vmem((NZ // 2, TILE, 128), BF16),
        vmem((TILE, 128), BF16),
        vmem((NDUO, TILE, 128), BF16),
        vmem((NX * NCHAN, TILE, 128), BF16),
        vmem((NQUAD, TILE, 128), BF16),
        vmem((TILE, 128), BF16),
        vmem((NZ // 2, TILE, 128), BF16),
        vmem((TILE, 128), BF16),
        vmem((NX, TILE, 128), BF16),
        dma((8,)),
        dma((6, 2)),
        dma((6, 2)),
        dma((EXCHANGES,)),
        dma((EXCHANGES,)),
    ]
    results = (
        shape((OUT_PART, ROWS_DEV), BF16),
        shape((GROUP, PIX), F32),
        shape((ORDER * GROUP, 128), F32),
        shape((128, 128), F32),
        shape((OUTF, 128), F32),
    )
    found = pl.pallas_call(
        kernel,
        out_shape=results,
        in_specs=[pl.BlockSpec(memory_space=pl.ANY)] * 8,
        out_specs=[pl.BlockSpec(memory_space=vmem)] * 5,
        scratch_shapes=scratch,
        compiler_params=pltpu.CompilerParams(
            collective_id=0, has_side_effects=True, vmem_limit_bytes=60 * 1024 * 1024
        ),
        cost_estimate=pl.CostEstimate(
            flops=600_000_000, bytes_accessed=1_000_000, transcendentals=65_536
        ),
    )(*args)
    mlp_out, input_grad, cheb_grad, first_grad, second_grad = pl.pallas_call(
        writer,
        out_shape=results,
        in_specs=[pl.BlockSpec(memory_space=vmem)] * 5,
        out_specs=[pl.BlockSpec(memory_space=vmem)] * 5,
        compiler_params=pltpu.CompilerParams(vmem_limit_bytes=60 * 1024 * 1024),
    )(*found)
    return mlp_out, input_grad, cheb_grad.reshape(ORDER, GROUP, 128), first_grad, second_grad.T


def solution(mesh):
    return jax.shard_map(
        body,
        mesh=mesh,
        in_specs=(
            P("chan", "region"),
            P(None, "region"),
            P(None, "region"),
            P(),
            P(None, "chan", None),
            P(None, "chan"),
            P("chan", None),
            P("chan", "region"),
        ),
        out_specs=(
            P("chan", "region"),
            P("chan", "region"),
            P(None, "chan", None),
            P(None, "chan"),
            P("chan", None),
        ),
        check_vma=False,
    )
```

```python
import math

import jax
import jax.numpy as jnp
from jax import lax
from jax.experimental import pallas as pl
from jax.experimental.pallas import tpu as pltpu
from jax.sharding import PartitionSpec as P

F32, BF16, I32 = jnp.float32, jnp.bfloat16, jnp.int32
MESH = pl.DeviceIdType.MESH
PIX, WW, ORDER, GROUP = 512, 128, 4, 32
NZ, NX, NXC, NCHAN, NREGION = 16, 4, 8, 4, 128
NPLANE = NXC * NCHAN
NDUO, TILE = 16, 16
OUT_PART, ROWS_DEV, OUTF = 16, 256, 64

W1, W2, W3, A1, A2, C0, DG, GS, B1, B2, G1, G2, F2, H1, H2, I2 = [*range(6), *range(9, 19)]
EXCHANGES = 19


def dot(left, right, left_dim=1, right_dim=0):
    return lax.dot_general(
        left, right, (((left_dim,), (right_dim,)), ((), ())), preferred_element_type=F32
    )


def iota(shape, dim):
    return lax.broadcasted_iota(I32, shape, dim)


def kernel(
    sky_in, nb_in, sl_in, cnt_in, cheb_in, w1_in, w2_in, cot_in,
    mo_out, ig_out, cg_out, fg_out, sg_out,
    sky, nb, sl, cnt, cheb, w1, w2, cot,
    amat, smat, mmat, emat, basis, hs, hr, wg1, wg2, s1, r1, s2, r2, wt, wgt, bs, bq,
    dg_s, dg, gs, gr, g1, rg1, g2, rg2, ft, fin, h1, rh1, h2, rh2, fs, fins,
    loads, hsend, hrecv, send, recv, h1send,
):
    region, chan = lax.axis_index("region"), lax.axis_index("chan")
    core, z, x = lax.rem(region, 2), lax.rem(lax.div(region, 2), NZ), lax.div(region, 2 * NZ)
    xc = x * 2 + core

    plane = xc * NCHAN + chan

    def z_peer(step):
        other = lax.rem(z + step, NZ)
        return other, ((x * NZ + other) * 2 + core, chan)

    def plane_peer(step):
        other = lax.rem(plane + step, NPLANE)
        there = lax.div(other, NCHAN)
        there = (lax.div(there, 2) * NZ + z) * 2 + lax.rem(there, 2)
        return other, (there, lax.rem(other, NCHAN))

    parity, z_pair = lax.rem(z, 2), lax.div(z, 2)
    duo = xc * 2 + parity
    holder = duo == x * 4

    def duo_device(other):
        there = lax.div(other, 4) * NZ + z_pair * 2 + lax.rem(other, 2)
        return there * 2 + lax.rem(lax.div(other, 2), 2), chan

    def duo_peer(step):
        other = lax.rem(duo + step, NDUO)
        return other, duo_device(other)

    def line_peer(step):
        other = lax.rem(z_pair + step, NZ // 2)
        return other, ((x * NZ + other * 2 + parity) * 2 + core, chan)

    def chan_peer(step):
        other = lax.rem(chan + step, NCHAN)
        return other, (region, other)

    lower = (lax.rem(region + NREGION - 1, NREGION), chan)
    upper = (lax.rem(region + 1, NREGION), chan)

    barrier = pltpu.get_barrier_semaphore()

    def greet(peer, count):
        def step(d, carry):
            pl.semaphore_signal(barrier, inc=1, device_id=peer(d)[1], device_id_type=MESH)
            return carry

        lax.fori_loop(1, count, step, 0)

    greet(z_peer, NZ)
    for device in (lower, upper):
        pl.semaphore_signal(barrier, inc=1, device_id=device, device_id_type=MESH)
    greet(duo_peer, NDUO)
    greet(plane_peer, NPLANE)

    pairs = (
        (nb_in, nb), (sl_in, sl), (sky_in, sky), (cnt_in, cnt),
        (cot_in, cot), (w1_in, w1), (w2_in, w2), (cheb_in, cheb),
    )
    load = {id(there): pltpu.make_async_copy(here, there, loads.at[i]) for i, (here, there) in enumerate(pairs)}
    for copy in load.values():
        copy.start()

    def loaded(*refs):
        for ref in refs:
            load[id(ref)].wait()

    def spread(key, peer, count, src_at, dst):
        def step(d, carry):
            slot, device = peer(d)
            pltpu.make_async_remote_copy(
                src_ref=src_at(slot), dst_ref=dst, send_sem=send.at[key],
                recv_sem=recv.at[key], device_id=device, device_id_type=MESH,
            ).start()
            return carry

        lax.fori_loop(1, count, step, 0)

    def await_bytes(ref, sem):
        pltpu.make_async_copy(ref, ref, sem).wait()

    loaded(nb, sl, sky)
    links = nb[...]
    inv = 1.0 / jnp.sqrt(
        jnp.maximum(jnp.sum((links != PIX + 2 * WW).astype(F32), axis=0, keepdims=True), 1.0)
    )
    slot_row = iota((PIX, WW), 0)
    for side in range(2):
        smat[:, side * WW : (side + 1) * WW] = (
            jnp.where(slot_row == sl[side : side + 1, :], 1.0, 0.0).astype(BF16)
        )

    def halo_copy(step, side):
        return pltpu.make_async_remote_copy(
            src_ref=hs.at[step, side], dst_ref=hr.at[step, 1 - side],
            send_sem=hsend.at[step, side], recv_sem=hrecv.at[step, 1 - side],
            device_id=(lower, upper)[side], device_id_type=MESH,
        )

    def rim(step, values):
        scaled = values * inv
        high = scaled.astype(BF16)
        edge = dot(high, smat[...]).astype(BF16)
        hs[step, 0] = edge[:, :WW]
        hs[step, 1] = edge[:, WW:]
        return scaled, high

    def halo_start(step):
        for side in range(2):
            halo_copy(step, side).start()

    def inner(pair):
        scaled, high = pair
        low = (scaled - high.astype(F32)).astype(BF16)
        both = dot(jnp.concatenate([high, low], axis=0), amat[:PIX])
        return both[:GROUP] + both[GROUP:]

    def finish(step, local):
        for side in range(2):
            halo_copy(step, 1 - side).wait_recv()
        local = local + dot(hr[step, 0], amat[PIX : PIX + WW])
        local = local + dot(hr[step, 1], amat[PIX + WW :])
        return -inv * local

    def keep(level, values):
        basis[level * GROUP : (level + 1) * GROUP] = values
        for s in range(NCHAN):
            bs[level, s] = values[:, s * WW : (s + 1) * WW]

    def share(level):
        spread(C0 + level, chan_peer, NCHAN, lambda slot: bs.at[level, slot], bq.at[chan, level])
        bq[chan, level] = bs[level, chan]

    v0 = sky[...].astype(F32)
    keep(0, sky[...])
    pair = rim(0, v0)

    loaded(cnt, cot)
    counts = cnt[...].astype(F32)
    own_start = jnp.sum(
        jnp.where(iota((64, NREGION), 1) < region, counts, 0.0), axis=1, keepdims=True
    )[:1].astype(I32)

    def places(order):
        lane = iota(order.shape, 1)
        count = jnp.sum(jnp.where(lane == order, counts, 0.0), axis=1, keepdims=True).astype(I32)
        start = jnp.sum(jnp.where(lane < order, counts, 0.0), axis=1, keepdims=True).astype(I32)
        off = (region - start) & (NREGION - 1)
        first = (start + off - region) >> 7
        return count, off, first

    def exchange1(k, message):
        s1[k] = message.reshape(NZ, NX, 128)

    def exchange1_start(k, key):
        spread(key, z_peer, NZ, lambda slot: s1.at[k, slot], r1.at[k, z])
        r1[k, z] = s1[k, z]

    def exchange2(k, key1, key2):
        await_bytes(r1.at[k, pl.ds(0, NZ - 1)], recv.at[key1])
        here = jnp.concatenate([r1[k, :, i, :] for i in range(NX)], axis=0).astype(BF16)
        moved = dot(here, emat[...]).astype(BF16)
        for i in range(NX):
            for b in range(2 * NCHAN):
                s2[k, i * 2 * NCHAN + b] = moved[i * NZ : (i + 1) * NZ, b * 128 : (b + 1) * 128]
        spread(key2, plane_peer, NPLANE, lambda slot: s2.at[k, slot], r2.at[k, plane])
        r2[k, plane] = s2[k, plane]

    def arrived2(k, key2):
        await_bytes(r2.at[k, pl.ds(0, NPLANE - 1)], recv.at[key2])
        parts = r2[k].astype(F32).reshape(NXC, NCHAN, NZ, 128)
        total = parts[:, 0]
        for s in range(1, NCHAN):
            total = total + parts[:, s]
        return total.reshape(NREGION, 128).T.astype(BF16)

    pair_row = iota((NZ * NX, NREGION), 0)
    zmajor = ((pair_row & 3) * NZ + (pair_row >> 2)) * 2
    count0, off0, first0 = places(zmajor)
    count1, off1, first1 = places(zmajor + 1)
    own_cot = cot[...].astype(F32)
    shifted = [own_cot] + [pltpu.roll(own_cot, ROWS_DEV - s, 1) for s in range(1, 4)]
    shifted = jnp.concatenate(shifted, axis=0).astype(BF16)
    empty = jnp.zeros_like(shifted)
    shifted = jnp.concatenate(
        [jnp.concatenate([shifted, empty], axis=1), jnp.concatenate([empty, shifted], axis=1)], axis=0
    )
    own_row = iota((NZ * NX, ROWS_DEV), 1)
    choice = jnp.concatenate([own_row == first0, own_row == first1], axis=1)
    message = dot(jnp.where(choice, 1.0, 0.0).astype(BF16), shifted, 1, 1)
    lane64 = iota((NZ * NX, NREGION), 1)
    room = jnp.where(lane64 < 64, count0 - off0, count1 - off1)
    message = jnp.where(((lane64 & 63) >> 4) * NREGION < room, message, 0.0)
    exchange1(0, message)
    gone = jnp.where(region == 0, 0, -1)
    gone_up = jnp.where(region == NREGION - 1, 0, -1)
    links = jnp.where((links >= PIX) & (links < PIX + WW) & (gone == 0), PIX + 2 * WW, links)
    links = jnp.where((links >= PIX + WW) & (gone_up == 0), PIX + 2 * WW, links)
    block_row = iota((32, PIX), 0)

    def build(b, carry):
        base = pl.multiple_of(b * 32, 32)
        near = links - base
        total = jnp.zeros((32, PIX), F32)
        for e in range(8):
            total = total + jnp.where(block_row == near[e : e + 1], 1.0, 0.0)
        amat[pl.ds(base, 32), :] = total.astype(BF16)
        return carry

    lax.fori_loop(0, (PIX + 2 * WW) // 32, build, 0)

    pl.semaphore_wait(barrier, 2 + (NPLANE - 1) + (NZ - 1) + (NDUO - 1))
    exchange1_start(0, A1)
    halo_start(0)
    loaded(w1, w2)
    spread(W1, chan_peer, NCHAN, lambda slot: w1, wg1.at[chan])
    spread(W2, chan_peer, NCHAN, lambda slot: w2, wg2.at[chan])

    loaded(cheb)
    weight = cheb[...]
    wt[...] = weight.astype(F32).T.astype(BF16)
    spread(W3, chan_peer, NCHAN, lambda slot: wt, wgt.at[chan])
    wg1[chan] = w1[...]
    wg2[chan] = w2[...]
    wgt[chan] = wt[...]

    share(0)
    local = inner(pair)
    from_row, to_lane = iota((128, 1024), 0), iota((128, 1024), 1)
    emat[...] = jnp.where(
        ((from_row >> 4) == (to_lane >> 7))
        & ((to_lane & 127) == chan * OUT_PART + (from_row & 15)),
        1.0, 0.0,
    ).astype(BF16)
    lane, row = iota((NREGION, NREGION), 1), iota((NREGION, NREGION), 0)
    xcmajor = (((row >> 5) * NZ + (row & 15)) * 2) + ((row >> 4) & 1)
    to_pixels = jnp.where(((xcmajor - own_start) & 127) == lane, 1.0, 0.0).astype(BF16)
    to_rows = jnp.concatenate(
        [((zmajor + i - own_start) & 127) == lane64 for i in range(2)], axis=1
    )
    to_rows = jnp.where(to_rows, 1.0, 0.0).astype(BF16)
    v1 = finish(0, local)
    pair = rim(1, v1)
    halo_start(1)
    keep(1, v1.astype(BF16))
    share(1)
    local = inner(pair)
    v2 = 2.0 * finish(1, local) - v0
    pair = rim(2, v2)
    halo_start(2)
    keep(2, v2.astype(BF16))
    share(2)
    local = inner(pair)
    exchange2(0, A1, A2)
    v3 = 2.0 * finish(2, local) - v1
    keep(3, v3.astype(BF16))
    share(3)

    await_bytes(wg2.at[pl.ds(0, NCHAN - 1)], recv.at[W2])
    await_bytes(wg1.at[pl.ds(0, NCHAN - 1)], recv.at[W1])
    await_bytes(wgt.at[pl.ds(0, NCHAN - 1)], recv.at[W3])
    for level in range(ORDER):
        await_bytes(bq.at[pl.ds(0, NCHAN - 1), level], recv.at[C0 + level])
    conv = jnp.zeros((128, WW), F32)
    for s in range(NCHAN):
        conv = conv + dot(wgt[s], bq[s].reshape(ORDER * GROUP, WW))
    features = conv.astype(BF16)
    features_t = conv.T.astype(BF16)
    hidden, slope = [], []
    out_t = jnp.zeros((WW, OUTF), F32)
    for h in range(NCHAN):
        pre = dot(features_t, wg1[h])
        gate = jax.nn.sigmoid(pre)
        hidden.append((pre * gate).astype(BF16))
        slope.append(gate * (1.0 + pre * (1.0 - gate)))

    columns = dot(arrived2(0, A2), to_pixels)[:OUTF]
    cot_px = columns.astype(BF16)
    cot_t = columns.T.astype(BF16)
    d_pre = []
    d_feat = jnp.zeros((WW, 128), F32)
    for h in range(NCHAN):
        d_pre.append((dot(cot_t, wg2[h]) * slope[h]).astype(BF16))
        d_feat = d_feat + dot(d_pre[h], wg1[h], 1, 1)
    dg_s[...] = d_feat.astype(BF16)
    spread(DG, chan_peer, NCHAN, lambda slot: dg_s, dg.at[chan])
    dg[chan] = dg_s[...]

    for h in range(NCHAN):
        gs[h, 0:128] = dot(features, d_pre[h]).astype(BF16)
        gs[h, 128:192] = dot(cot_px, hidden[h]).astype(BF16)
        out_t = out_t + dot(hidden[h], wg2[h], 1, 1)
    spread(GS, chan_peer, NCHAN, lambda slot: gs.at[slot], gr.at[chan])
    gr[chan] = gs[chan]
    outs = out_t.T.astype(BF16)
    empty = jnp.zeros_like(outs)
    outs = jnp.concatenate(
        [jnp.concatenate([outs, empty], axis=1), jnp.concatenate([empty, outs], axis=1)], axis=0
    )
    exchange1(1, dot(to_rows, outs, 1, 1))
    exchange1_start(1, B1)

    await_bytes(dg.at[pl.ds(0, NCHAN - 1)], recv.at[DG])
    d_conv_t = dg[...].reshape(PIX, 128)
    cheb_part = dot(basis[...], d_conv_t)
    for i in range(NXC):
        g1[2 * i] = cheb_part[TILE * i : TILE * (i + 1)].astype(BF16)

    def to_half(half):
        def step(d, carry):
            other = 2 * d + half

            @pl.when(other != duo)
            def _():
                pltpu.make_async_remote_copy(
                    src_ref=g1.at[other], dst_ref=rg1.at[duo], send_sem=send.at[G1],
                    recv_sem=recv.at[G1], device_id=duo_device(other), device_id_type=MESH,
                ).start()

            return carry

        lax.fori_loop(0, NDUO // 2, step, 0)

    to_half(0)
    adj3 = dot(weight[3 * GROUP :], d_conv_t, 1, 1)
    pair = rim(3, adj3)
    halo_start(3)
    await_bytes(gr.at[pl.ds(0, NCHAN - 1)], recv.at[GS])
    grads = gr[0].astype(F32)
    for s in range(1, NCHAN):
        grads = grads + gr[s].astype(F32)
    for i in range(NXC):
        g1[2 * i + 1] = grads[TILE * i : TILE * (i + 1)].astype(BF16)
    to_half(1)
    for i in range(NX):
        h1[i] = grads[128 + TILE * i : 128 + TILE * (i + 1)].astype(BF16)

    def to_holder(i):
        return pltpu.make_async_remote_copy(
            src_ref=h1.at[i], dst_ref=rh1.at[duo], send_sem=h1send.at[i], recv_sem=recv.at[H1],
            device_id=duo_device(4 * i), device_id_type=MESH,
        )

    for i in range(NX):
        @pl.when(duo != 4 * i)
        def _(i=i):
            to_holder(i).start()

        @pl.when(duo == 4 * i)
        def _(i=i):
            rh1[duo] = h1[i]

    rg1[duo] = g1[duo]
    local = inner(pair)
    d_low = dot(weight[: 3 * GROUP], d_conv_t, 1, 1)
    adj2 = d_low[2 * GROUP :] + 2.0 * finish(3, local)
    adj1 = d_low[GROUP : 2 * GROUP] - adj3
    pair = rim(4, adj2)
    halo_start(4)

    def sum_of(ref, count):
        total = ref[0].astype(F32)
        for s in range(1, count):
            total = total + ref[s].astype(F32)
        return total.astype(BF16)

    await_bytes(rg1.at[pl.ds(0, NDUO - 1)], recv.at[G1])
    g2[...] = sum_of(rg1, NDUO)
    spread(G2, line_peer, NZ // 2, lambda slot: g2, rg2.at[z_pair])
    rg2[z_pair] = g2[...]

    @pl.when(holder)
    def _():
        await_bytes(rh1.at[pl.ds(0, NDUO - 1)], recv.at[H1])
        h2[...] = sum_of(rh1, NDUO)
        spread(H2, line_peer, NZ // 2, lambda slot: h2, rh2.at[z_pair])
        rh2[z_pair] = h2[...]

    exchange2(1, B1, B2)
    local = inner(pair)
    count2, off2, first2 = places(xcmajor)
    out_row = iota((NREGION, ROWS_DEV), 1)
    for s in range(4):
        fine = (out_row == first2 + s) & (off2 + s * NREGION < count2)
        mmat[s] = jnp.where(fine, 1.0, 0.0).astype(BF16)
    adj1 = adj1 + 2.0 * finish(4, local)
    adj0 = d_low[:GROUP] - adj2
    pair = rim(5, adj1)
    halo_start(5)

    local = inner(pair)

    await_bytes(rg2.at[pl.ds(0, NZ // 2 - 1)], recv.at[G2])
    ft[...] = sum_of(rg2, NZ // 2)
    spread(F2, duo_peer, NDUO, lambda slot: ft, fin.at[duo])
    fin[duo] = ft[...]

    @pl.when(holder)
    def _():
        await_bytes(rh2.at[pl.ds(0, NZ // 2 - 1)], recv.at[H2])
        fs[...] = sum_of(rh2, NZ // 2)
        spread(I2, duo_peer, NDUO, lambda slot: fs, fins.at[x])
        fins[x] = fs[...]
        await_bytes(fins.at[pl.ds(0, NX - 1)], recv.at[I2])

    @pl.when(jnp.logical_not(holder))
    def _():
        await_bytes(fins, recv.at[I2])

    ig_out[...] = adj0 + finish(5, local)
    rows_t = arrived2(1, B2)
    result = jnp.zeros((OUT_PART, ROWS_DEV), F32)
    for s in range(4):
        result = result + dot(rows_t[s * OUT_PART : (s + 1) * OUT_PART], mmat[s])
    mo_out[...] = result.astype(BF16)

    scale = 1.0 / math.sqrt(NREGION * ROWS_DEV)
    await_bytes(fin.at[pl.ds(0, NDUO - 1)], recv.at[F2])
    for i in range(NXC):
        cg_out[TILE * i : TILE * (i + 1)] = fin[2 * i].astype(F32) * scale
        fg_out[TILE * i : TILE * (i + 1)] = fin[2 * i + 1].astype(F32) * scale
    sg_out[...] = fins[...].astype(F32).reshape(OUTF, 128) * scale

    for step in range(6):
        for side in range(2):
            halo_copy(step, side).wait_send()
    for key, ref in ((W1, wg1), (W2, wg2), (W3, wgt), (DG, dg), (GS, gr)):
        await_bytes(ref.at[pl.ds(0, NCHAN - 1)], send.at[key])
    for level in range(ORDER):
        await_bytes(bq.at[pl.ds(0, NCHAN - 1), level], send.at[C0 + level])
    for k, key1, key2 in ((0, A1, A2), (1, B1, B2)):
        await_bytes(r1.at[k, pl.ds(0, NZ - 1)], send.at[key1])
        await_bytes(r2.at[k, pl.ds(0, NPLANE - 1)], send.at[key2])
    await_bytes(rg1.at[pl.ds(0, NDUO - 1)], send.at[G1])
    await_bytes(rg2.at[pl.ds(0, NZ // 2 - 1)], send.at[G2])
    await_bytes(fin.at[pl.ds(0, NDUO - 1)], send.at[F2])
    for i in range(NX):
        @pl.when(duo != 4 * i)
        def _(i=i):
            to_holder(i).wait_send()

    @pl.when(holder)
    def _():
        await_bytes(rh2.at[pl.ds(0, NZ // 2 - 1)], send.at[H2])
        await_bytes(rh1.at[pl.ds(0, NDUO - 1)], send.at[I2])


def writer(*refs):
    count = len(refs) // 2
    for i in range(count):
        refs[count + i][...] = refs[i][...]


def body(
    sky_maps, neighbours, send_lists, counts, cheb_weight, first_weight, second_weight, cotangent
):
    dma = pltpu.SemaphoreType.DMA
    vmem = pltpu.VMEM
    shape = jax.ShapeDtypeStruct
    args = (
        sky_maps,
        neighbours,
        send_lists,
        counts.reshape(1, NREGION),
        cheb_weight.reshape(ORDER * GROUP, 128),
        first_weight,
        second_weight.T,
        cotangent,
    )
    scratch = [vmem(arg.shape, arg.dtype) for arg in args] + [
        vmem((PIX + 2 * WW, PIX), BF16),
        vmem((PIX, 2 * WW), BF16),
        vmem((4, NREGION, ROWS_DEV), BF16),
        vmem((128, 1024), BF16),
        vmem((ORDER * GROUP, PIX), BF16),
        vmem((6, 2, GROUP, WW), BF16),
        vmem((6, 2, GROUP, WW), BF16),
        vmem((NCHAN, 128, 128), BF16),
        vmem((NCHAN, OUTF, 128), BF16),
        vmem((2, NZ, NX, 128), F32),
        vmem((2, NZ, NX, 128), F32),
        vmem((2, NPLANE, NZ, 128), BF16),
        vmem((2, NPLANE, NZ, 128), BF16),
        vmem((128, ORDER * GROUP), BF16),
        vmem((NCHAN, 128, ORDER * GROUP), BF16),
        vmem((ORDER, NCHAN, GROUP, WW), BF16),
        vmem((NCHAN, ORDER, GROUP, WW), BF16),
        vmem((WW, 128), BF16),
        vmem((NCHAN, WW, 128), BF16),
        vmem((NCHAN, 192, 128), BF16),
        vmem((NCHAN, 192, 128), BF16),
        vmem((NDUO, TILE, 128), BF16),
        vmem((NDUO, TILE, 128), BF16),
        vmem((TILE, 128), BF16),
        vmem((NZ // 2, TILE, 128), BF16),
        vmem((TILE, 128), BF16),
        vmem((NDUO, TILE, 128), BF16),
        vmem((NX, TILE, 128), BF16),
        vmem((NDUO, TILE, 128), BF16),
        vmem((TILE, 128), BF16),
        vmem((NZ // 2, TILE, 128), BF16),
        vmem((TILE, 128), BF16),
        vmem((NX, TILE, 128), BF16),
        dma((8,)),
        dma((6, 2)),
        dma((6, 2)),
        dma((EXCHANGES,)),
        dma((EXCHANGES,)),
        dma((NX,)),
    ]
    results = (
        shape((OUT_PART, ROWS_DEV), BF16),
        shape((GROUP, PIX), F32),
        shape((ORDER * GROUP, 128), F32),
        shape((128, 128), F32),
        shape((OUTF, 128), F32),
    )
    found = pl.pallas_call(
        kernel,
        out_shape=results,
        in_specs=[pl.BlockSpec(memory_space=pl.ANY)] * 8,
        out_specs=[pl.BlockSpec(memory_space=vmem)] * 5,
        scratch_shapes=scratch,
        compiler_params=pltpu.CompilerParams(
            collective_id=0, has_side_effects=True, vmem_limit_bytes=60 * 1024 * 1024
        ),
        cost_estimate=pl.CostEstimate(
            flops=600_000_000, bytes_accessed=1_000_000, transcendentals=65_536
        ),
    )(*args)
    mlp_out, input_grad, cheb_grad, first_grad, second_grad = pl.pallas_call(
        writer,
        out_shape=results,
        in_specs=[pl.BlockSpec(memory_space=vmem)] * 5,
        out_specs=[pl.BlockSpec(memory_space=vmem)] * 5,
        compiler_params=pltpu.CompilerParams(vmem_limit_bytes=60 * 1024 * 1024),
    )(*found)
    return mlp_out, input_grad, cheb_grad.reshape(ORDER, GROUP, 128), first_grad, second_grad.T


def solution(mesh):
    return jax.shard_map(
        body,
        mesh=mesh,
        in_specs=(
            P("chan", "region"),
            P(None, "region"),
            P(None, "region"),
            P(),
            P(None, "chan", None),
            P(None, "chan"),
            P("chan", None),
            P("chan", "region"),
        ),
        out_specs=(
            P("chan", "region"),
            P("chan", "region"),
            P(None, "chan", None),
            P(None, "chan"),
            P("chan", None),
        ),
        check_vma=False,
    )
```
